32 devices in a mesh: space: 16 (over z, y, x), members: 2 (over core).
Axes of the slice: x: 2, y: 2, z: 4, core: 2. Of those that a mesh axis runs over, the one named last changes fastest.
Arguments:
- log_field: float32 [128, 2048], P('members', 'space'), may hold values from -6 to 6
- obs_heads: float32 [512], P('space'), may hold values from -6 to 6
- obs_var: float32 [512], P('space'), may hold values from 0.05 to 0.5
- obs_noise: float32 [128, 512], P('members', 'space'), may hold values from -6 to 6
- obs_index: int32 [16, 32], P('space'), may hold values from 0 to 127
- obs_count: int32 [16], P('space'), may hold values from 1 to 32, 256 in all
- neighbours: int32 [128, 64], P('members'), may hold values from 0 to 127, all different within a row
- lift_gain: float32 [48], replicated, may hold values from -4 to 4
- lift_bias: float32 [48], replicated, may hold values from -3 to 3
- conv_first: bfloat16 [3, 48, 48], replicated, may hold values from -0.5 to 0.5
- bias_first: float32 [48], replicated, may hold values from -2 to 2
- conv_second: bfloat16 [3, 48, 96], replicated, may hold values from -0.375 to 0.375
- bias_second: float32 [48], replicated, may hold values from -2 to 2
- readout: bfloat16 [144], replicated, may hold values from -0.5 to 0.5
Outputs:
- updated_field: float32 [128, 2048], P('members', 'space')
- new_heads: float32 [128, 2048], P('members', 'space')
The draws below stay inside these ranges and needn't reach their ends.
Inputs may be any that keep to these rules, and one draw needn't show every extreme that they name: `obs_index`: cells are counted within the tile that holds the slot. `obs_count`: the counts sum to 256 and the largest is exactly 32. `neighbours`: each row names 64 different members; every member is named by some row.
All inputs are finite; a program needn't handle non-finite values. No bound on the sum of `obs_count` on one device may be relied on, other than what follows from the above.
Results may differ from the reference program's by a relative error of at most 0.0051.
Values may be sent and summed in bfloat16 or wider, within the bound.
No kernel may reach another device: no remote copies, remote signals or barrier semaphores. Data moves between devices by JAX's collectives and lax.ppermute only.
A program may use at most 64 MiB of HBM per device.

```python
import math
import jax
import jax.numpy as jnp
import numpy as np
from jax import lax

CHANNELS = 48
NEIGHBOURS = 64
CELLS_DEV = 128
OBS_CAP = 32
MEMBERS = 128
CELLS = 2048
OBS_TOTAL = 512
N_SPACE = 16


def with_ends(values, rng, low, top_value):
    longest = values.shape.index(max(values.shape))
    spots = []
    for shift in (0, 1):
        where = [jax.random.randint(jax.random.fold_in(rng, axis), (), 0, length) for axis, length in enumerate(values.shape)]
        where[longest] = (where[longest] + shift) % values.shape[longest]
        spots.append(tuple(where))
    return values.at[spots[0]].set(low).at[spots[1]].set(top_value)


def block_scale(key, extent, cuts, smallest, largest):
    factor_of = 1.0
    for position, parts in cuts:
        draws = jax.random.uniform(jax.random.fold_in(jax.random.fold_in(key, 6), position), (parts,), jnp.float32, smallest / len(cuts), largest / len(cuts))
        factor_of = factor_of * jnp.repeat(jnp.exp(draws), extent[position] // parts).reshape((-1,) + (1,) * (len(extent) - 1 - position))
    return factor_of


def different_ones(own_key, rows, number_of, top, lift):
    order = jax.random.permutation(jax.random.fold_in(own_key, 1), number_of)
    favour = order
    for power in range(3):
        favour = favour * favour // number_of
    favour = favour * lift // number_of
    tickets = jax.random.randint(jax.random.fold_in(own_key, 2), (rows, number_of), 0, 4096) + favour
    sure = jax.random.permutation(jax.random.fold_in(own_key, 3), rows)[jnp.arange(number_of) % rows]
    tickets = jnp.where(jnp.arange(rows)[:, None] == sure[None, :], 1 << 14, tickets)
    score = tickets * number_of + jnp.arange(number_of)
    return lax.top_k(score.astype(jnp.int32), top)[1].astype(jnp.int32)


def split_up(amount, total, bound, skew):
    loads = [(1 << 20) // math.isqrt(rank ** skew) + 1 for rank in range(2, amount + 1)]
    spare, counts = total - bound - (amount - 1), [1] * (amount - 1)
    while spare > 0:
        free = [i for i in range(amount - 1) if counts[i] < bound]
        pool, left = sum([loads[i] for i in free]), spare
        for i in free:
            addition = min(bound - counts[i], max(1, left * loads[i] // pool), spare)
            counts[i] = counts[i] + addition
            spare = spare - addition
    return np.array([bound] + counts)


def uneven(own_key, count, total, reach, slope):
    if count == 2:
        one = jax.random.randint(own_key, (), max(1, total - reach), min(reach, total - 1) + 1)
        return jnp.stack([one, total - one])
    sizes = jnp.asarray(split_up(count, total, reach, slope), jnp.int32)
    couples = (count - 1) // 2
    donor, taker = sizes[1:1 + 2 * couples:2], sizes[2:2 + 2 * couples:2]
    slack = jnp.minimum(donor - 1, reach - taker)
    shifted = jax.random.randint(jax.random.fold_in(own_key, 1), (couples,), 0, 1 << 20) % (slack + 1)
    sizes = sizes.at[1:1 + 2 * couples:2].set(donor - shifted).at[2:2 + 2 * couples:2].set(taker + shifted)
    return sizes[jax.random.permutation(jax.random.fold_in(own_key, 2), count)]


def scatter_about(key, shape, width, bound, pieces=(), held_as=jnp.bfloat16):
    drawn = width * jax.random.normal(key, shape, jnp.float32)
    if pieces:
        drawn = drawn * block_scale(key, shape, pieces, -0.22, 0.18)
    return jnp.clip(drawn, -bound, bound).astype(held_as)


def setup_inputs(seed: int = 0) -> dict:
    splits = jax.random.split(jax.random.key(seed), 15)
    return {
        "log_field": scatter_about(splits[0], (MEMBERS, CELLS), 1.0, 6.0, ((0, 2), (1, 16)), jnp.float32),
        "obs_heads": scatter_about(splits[1], (OBS_TOTAL,), 1.0, 6.0, ((0, 16),), jnp.float32),
        "obs_var": jnp.clip(jnp.exp(math.log(0.5) - 2.3025851 * jax.random.uniform(splits[2], (OBS_TOTAL,), jnp.float32) ** block_scale(splits[2], (OBS_TOTAL,), ((0, 16),), -0.2, 0.2)), 0.05, 0.5),
        "obs_noise": scatter_about(splits[3], (MEMBERS, OBS_TOTAL), 1.0, 6.0, ((0, 2), (1, 16)), jnp.float32),
        "obs_index": with_ends(jax.random.randint(splits[4], (N_SPACE, OBS_CAP), 0, CELLS_DEV), jax.random.fold_in(splits[4], 1), 0, CELLS_DEV - 1).astype(jnp.int32),
        "obs_count": uneven(splits[5], N_SPACE, OBS_TOTAL // 2, OBS_CAP, 2).astype(jnp.int32),
        "neighbours": different_ones(splits[6], MEMBERS, MEMBERS, NEIGHBOURS, 8192),
        "lift_gain": scatter_about(splits[7], (CHANNELS,), 1.0, 4.0, (), jnp.float32),
        "lift_bias": scatter_about(splits[8], (CHANNELS,), 0.5, 3.0, (), jnp.float32),
        "conv_first": scatter_about(splits[9], (3, CHANNELS, CHANNELS), (3 * CHANNELS) ** -0.5, 0.5),
        "bias_first": scatter_about(splits[10], (CHANNELS,), 0.3, 2.0, (), jnp.float32),
        "conv_second": scatter_about(splits[11], (3, CHANNELS, 2 * CHANNELS), (6 * CHANNELS) ** -0.5, 0.375),
        "bias_second": scatter_about(splits[12], (CHANNELS,), 0.3, 2.0, (), jnp.float32),
        "readout": scatter_about(splits[13], (3 * CHANNELS,), (3 * CHANNELS) ** -0.5, 0.5),
    }


def dilated_conv(padded_input, kernel_taps, kernel_bias, dilation, width_cells):
    total_sum = jnp.zeros((kernel_taps.shape[1], padded_input.shape[1], width_cells), jnp.float32)
    for kernel_tap in range(3):
        window_cells = lax.slice_in_dim(padded_input, kernel_tap * dilation, kernel_tap * dilation + width_cells, axis=2)
        total_sum = total_sum + jnp.einsum('oc,cmn->omn', kernel_taps[kernel_tap].astype(jnp.float32), window_cells.astype(jnp.float32), precision=lax.Precision.HIGHEST)
    return jax.nn.silu(total_sum + kernel_bias[:, None, None])

def surrogate_block(member_rows, lift_gain, lift_bias, conv_first, bias_first, conv_second, bias_second, readout):
    width_cells = member_rows.shape[1]
    channels = lift_gain.shape[0]
    first_layer = jnp.tanh(lift_gain[:, None, None] * member_rows[None] + lift_bias[:, None, None]).astype(jnp.bfloat16)
    padded_first = jnp.pad(first_layer, ((0, 0), (0, 0), (1, 1)))
    second_layer = dilated_conv(padded_first, conv_first, bias_first, 1, width_cells).astype(jnp.bfloat16)
    joined_layers = jnp.concatenate([first_layer, second_layer], axis=0)
    padded_joined = jnp.pad(joined_layers, ((0, 0), (0, 0), (2, 2)))
    third_layer = dilated_conv(padded_joined, conv_second, bias_second, 2, width_cells).astype(jnp.bfloat16)
    readout_wide = readout.astype(jnp.float32)
    result = jnp.einsum('c,cmn->mn', readout_wide[:channels], first_layer.astype(jnp.float32), precision=lax.Precision.HIGHEST)
    result = result + jnp.einsum('c,cmn->mn', readout_wide[channels:2 * channels], second_layer.astype(jnp.float32), precision=lax.Precision.HIGHEST)
    result = result + jnp.einsum('c,cmn->mn', readout_wide[2 * channels:], third_layer.astype(jnp.float32), precision=lax.Precision.HIGHEST)
    return result

def surrogate(log_values, lift_gain, lift_bias, conv_first, bias_first, conv_second, bias_second, readout):
    blocks = log_values.reshape(MEMBERS // 16, 16, CELLS)

    def one_block(block_rows):
        return surrogate_block(block_rows, lift_gain, lift_bias, conv_first, bias_first, conv_second, bias_second, readout)
    return lax.map(one_block, blocks).reshape(MEMBERS, CELLS)

def gram_terms(neighbour_rows, innov_rows, obs_weight):
    anomaly = neighbour_rows - lax.optimization_barrier(jnp.mean(neighbour_rows, axis=1, keepdims=True))
    scaled = anomaly * obs_weight
    gram = jnp.einsum('bko,blo->bkl', scaled, anomaly, precision=lax.Precision.HIGHEST)
    rhs = jnp.einsum('bko,bo->bk', scaled, innov_rows, precision=lax.Precision.HIGHEST)
    return (gram, rhs)

def solve_weights(gram, rhs):
    order = gram.shape[-1]
    system = gram + (order - 1.0) * jnp.eye(order, dtype=gram.dtype)
    factor = jnp.linalg.cholesky(system)
    half_solved = jax.scipy.linalg.solve_triangular(factor, rhs[..., None], lower=True)
    solved = jax.scipy.linalg.solve_triangular(factor, half_solved, lower=True, trans=1)[..., 0]
    return solved - lax.optimization_barrier(jnp.mean(solved, axis=-1, keepdims=True))

def reference(log_field, obs_heads, obs_var, obs_noise, obs_index, obs_count, neighbours, lift_gain, lift_bias, conv_first, bias_first, conv_second, bias_second, readout):
    heads = surrogate(log_field, lift_gain, lift_bias, conv_first, bias_first, conv_second, bias_second, readout)
    tile_start = (jnp.arange(N_SPACE, dtype=jnp.int32) * CELLS_DEV)[:, None]
    cell_ids = (obs_index.astype(jnp.int32) + tile_start).reshape(-1)
    predicted = jnp.take(heads, cell_ids, axis=1)
    live_slots = (jnp.arange(OBS_CAP, dtype=jnp.int32)[None, :] < obs_count.astype(jnp.int32)[:, None]).reshape(-1)
    obs_weight = jnp.where(live_slots, 1.0 / obs_var, jnp.zeros_like(obs_var))
    innovation = obs_heads[None, :] + jnp.sqrt(obs_var)[None, :] * obs_noise - predicted

    def block_solve(block_args):
        member_ids, innov_rows = block_args
        gram, rhs = gram_terms(jnp.take(predicted, member_ids, axis=0), innov_rows, obs_weight)
        return solve_weights(gram, rhs)
    coef = lax.map(block_solve, (neighbours.reshape(MEMBERS // 16, 16, NEIGHBOURS), innovation.reshape(MEMBERS // 16, 16, OBS_TOTAL))).reshape(MEMBERS, NEIGHBOURS)
    row_ids = jnp.arange(MEMBERS, dtype=jnp.int32)[:, None]
    mixing = jnp.zeros((MEMBERS, MEMBERS), log_field.dtype).at[row_ids, neighbours.astype(jnp.int32)].add(coef)
    updated_field = log_field + jnp.dot(mixing, log_field, precision=lax.Precision.HIGHEST)
    new_heads = surrogate(updated_field, lift_gain, lift_bias, conv_first, bias_first, conv_second, bias_second, readout)
    return (updated_field, new_heads)
```

```python
import functools

import jax
import jax.numpy as jnp
from jax import lax
from jax.experimental import pallas as pl
from jax.experimental.pallas import tpu as pltpu
from jax.sharding import PartitionSpec as P

F32 = jnp.float32
BF16 = jnp.bfloat16
HALO = 3
EDGE = 8
PARTS = 4
VMEM = pl.BlockSpec(memory_space=pltpu.VMEM)
SMEM = pl.BlockSpec(memory_space=pltpu.SMEM)


def shape(dims, dtype=F32):
    return jax.ShapeDtypeStruct(dims, dtype)


def call(kernel, outs, args, in_specs=None, scratch=(), flops=0, limit=40):
    return pl.pallas_call(
        kernel,
        out_shape=outs,
        in_specs=in_specs or [VMEM] * len(args),
        out_specs=jax.tree.map(lambda _: VMEM, outs),
        scratch_shapes=list(scratch),
        cost_estimate=pl.CostEstimate(flops=flops, bytes_accessed=1 << 18, transcendentals=0),
        compiler_params=pltpu.CompilerParams(vmem_limit_bytes=limit << 20),
    )(*args)


def column(row):
    size = row.shape[1]
    same = lax.broadcasted_iota(jnp.int32, (size, size), 0) == lax.broadcasted_iota(
        jnp.int32, (size, size), 1
    )
    return jnp.sum(jnp.where(same, row, 0.0), axis=1, keepdims=True)


def pick(rows, group, width):
    own = rows[:, :width]
    for other in range(1, rows.shape[1] // width):
        own = jnp.where(group == other, rows[:, other * width : (other + 1) * width], own)
    return own


def edges_kernel(field, turned, low, high):
    value = field[...].T
    turned[...] = value
    low[...] = value[:EDGE]
    high[...] = value[value.shape[0] - EDGE :]


def weights_kernel(
    gain, bias, conv1, bias1, conv2, bias2, readout, neighbours,
    taps1, taps2, last, columns, near, near_turned, wide1, wide2,
):
    channels = gain.shape[0]
    for tap in range(3):
        wide1[:, tap * channels : (tap + 1) * channels] = 0.5 * conv1[tap].astype(F32)
    taps1[...] = wide1[...].astype(BF16)
    wide2[...] = jnp.zeros_like(wide2)
    both = 2 * channels
    for tap in range(3):
        wide2[0:channels, tap * both : (tap + 1) * both] = 0.5 * conv2[tap].astype(F32)
    row = readout[...].astype(F32).reshape(1, 3 * channels)
    wide2[channels : channels + 1, both : 2 * both] = row[:, :both]
    taps2[...] = wide2[...].astype(BF16)
    pad = jnp.zeros((last.shape[0] - 1, channels), F32)
    last[...] = jnp.concatenate([row[:, both:], pad], axis=0).astype(BF16)
    for spot, (source, factor) in enumerate(((gain, 1.0), (bias, 1.0), (bias1, 0.5), (bias2, 0.5))):
        col = column(source[...].astype(F32).reshape(1, channels)) * factor
        columns[spot] = jnp.broadcast_to(col, (channels, columns.shape[2]))
    ids = neighbours[...]
    pair = jnp.concatenate([ids, ids], axis=1)
    near[...] = jnp.concatenate([pair, pair], axis=0)
    near_turned[...] = pair.T


def surrogate(ext, space, taps1, taps2, last, columns, first, second, heads, turned):
    spaces = lax.axis_size("space")
    cells = ext.shape[0] - 2 * HALO
    members = ext.shape[1]
    run = cells // PARTS
    rows = run + 2 * HALO
    lanes = PARTS * members
    wide = jnp.concatenate([ext[q * run : q * run + rows] for q in range(PARTS)], axis=1)
    gain, bias, bias1, bias2 = [
        jnp.concatenate([columns[i]] * (lanes // columns.shape[2]), axis=1) for i in range(4)
    ]
    channels = gain.shape[0]
    lane = lax.broadcasted_iota(jnp.int32, (1, lanes), 1)
    left = jnp.where((lane < members) & (space == 0), 0.0, 1.0)
    right = jnp.where((lane >= lanes - members) & (space == spaces - 1), 0.0, 1.0)
    for r in range(rows):
        value = jnp.tanh(gain * wide[r : r + 1] + bias)
        if r < HALO:
            value = value * left
        if r >= rows - HALO:
            value = value * right
        first[r] = value.astype(BF16)
    for i in range(rows - 2):
        window = first[i : i + 3].reshape(3 * channels, lanes)
        half = jnp.dot(taps1[...], window, preferred_element_type=F32) + bias1
        value = half + half * jnp.tanh(half)
        if i < HALO - 1:
            value = value * left
        if i >= rows - 2 - (HALO - 1):
            value = value * right
        second[i] = value.astype(BF16)
    for n in range(run):
        window = jnp.concatenate(
            [first[n + 1], second[n], first[n + 3], second[n + 2], first[n + 5], second[n + 4]],
            axis=0,
        )
        total = jnp.dot(taps2[...], window, preferred_element_type=F32)
        half = total[:channels] + bias2
        third = (half + half * jnp.tanh(half)).astype(BF16)
        rest = jnp.dot(last[...], third, preferred_element_type=F32)
        heads[n : n + 1, :] = total[channels : channels + 1] + rest[0:1]
    for q in range(PARTS):
        turned[q * run : (q + 1) * run, :] = heads[:, q * members : (q + 1) * members]


def observe_kernel(
    field, from_left, from_right, taps1, taps2, last, columns,
    obs_heads, obs_var, obs_noise, obs_index, obs_count,
    sent, first, second, heads, turned, chosen,
):
    space = lax.axis_index("space")
    group = lax.axis_index("members")
    members = field.shape[0]
    own = field[...].T
    ext = jnp.concatenate(
        [
            pick(from_left[...], group, members)[EDGE - HALO :],
            own,
            pick(from_right[...], group, members)[:HALO],
        ],
        axis=0,
    )
    surrogate(ext, space, taps1, taps2, last, columns, first, second, heads, turned)
    slots = obs_var.shape[0]
    for k in range(slots):
        chosen[k : k + 1, :] = turned[pl.ds(obs_index[0, k], 1), :]
    own_obs = chosen[...]
    target = column(obs_heads[...].reshape(1, slots))
    variance = column(obs_var[...].reshape(1, slots))
    live = lax.broadcasted_iota(jnp.int32, (slots, 1), 0) < obs_count[0]
    root = jnp.where(live, lax.rsqrt(variance), 0.0)
    innovation = target + jnp.sqrt(variance) * obs_noise[...].T - own_obs
    payload = jnp.concatenate([root * own_obs, root * innovation], axis=1)
    for copy in range(sent.shape[0]):
        sent[copy] = payload


def split3(value):
    one = value.astype(BF16)
    rest = value - one.astype(F32)
    two = rest.astype(BF16)
    three = (rest - two.astype(F32)).astype(BF16)
    return jnp.concatenate([one, two, three], axis=1)


def lane_gather(table, index):
    low = index & 127
    high = index >> 7
    found = None
    for tile in range(table.shape[1] // 128):
        part = jnp.take_along_axis(
            table[:, tile * 128 : (tile + 1) * 128], low, axis=1, mode="promise_in_bounds"
        )
        found = part if found is None else jnp.where(high == tile, part, found)
    return found


def update_kernel(
    got, field, turned_all, from_left, from_right, taps1, taps2, last, columns, near, near_turned,
    updated, new_heads,
    system, inverse, first, second, heads, turned,
):
    space = lax.axis_index("space")
    group = lax.axis_index("members")
    groups, slots = got.shape[0], got.shape[1] * got.shape[2]
    members = got.shape[3] // 2
    everyone = groups * members
    order = near.shape[0] // 2
    half_lane = lax.broadcasted_iota(jnp.int32, (1, 128), 1) < 64

    panel = jnp.concatenate(
        [got[g].reshape(slots, 2 * members)[:, :members] for g in range(groups)], axis=1
    )
    panel = panel - jnp.mean(panel, axis=1, keepdims=True)
    innovation = got[group].reshape(slots, 2 * members)[:, members:]
    stacked = jnp.concatenate([panel, innovation], axis=1)
    product = lax.dot_general(
        stacked, panel, (((0,), (0,)), ((), ())),
        precision=lax.Precision.HIGHEST, preferred_element_type=F32,
    )
    gram = split3(product[:everyone])
    sides = product[everyone:]

    ids = near[...]
    second_half = (lax.broadcasted_iota(jnp.int32, (128, 128), 0) >= 64).astype(jnp.int32)
    lane_id = lax.broadcasted_iota(jnp.int32, (128, 128), 1)
    row_id = lax.broadcasted_iota(jnp.int32, (128, 128), 0)
    everyone_id = lax.broadcasted_iota(jnp.int32, (128, everyone), 1)

    def extract(quad, carry):
        found = []
        for b in range(2):
            column_id = 4 * quad + 2 * b + second_half
            member = jnp.take_along_axis(ids, column_id, axis=1, mode="promise_in_bounds")
            member = jnp.concatenate([member] * (everyone // 128), axis=1)
            chosen = jnp.where(member == everyone_id, 1.0, 0.0).astype(BF16)
            parts = jnp.dot(chosen, gram, preferred_element_type=F32)
            rows = (
                parts[:, :everyone]
                + parts[:, everyone : 2 * everyone]
                + parts[:, 2 * everyone :]
            )
            found.append(lane_gather(rows, ids))
        block = jnp.where(half_lane, found[0], found[1]).T
        own = 4 * quad + 2 * (row_id >= 64).astype(jnp.int32) + (lane_id >= 64).astype(jnp.int32)
        block = block + jnp.where((row_id & 63) == own, order - 1.0, 0.0)
        system[pl.ds(pl.multiple_of(quad * 128, 128), 128), :] = block
        return carry

    lax.fori_loop(0, order // 4, extract, 0)
    side = lane_gather(jnp.concatenate([sides, sides], axis=0), ids)
    side = jnp.where(row_id >= 64, 1.0, side).T[:order]
    system[order // 2 * order : (order // 2 + 1) * order, :] = side

    blocks = order // 2
    level = lax.broadcasted_iota(jnp.int32, (order, 128), 0)

    def both(value):
        turn = pltpu.roll(value, 64, 1)
        return jnp.where(half_lane, value, turn), jnp.where(half_lane, turn, value)

    chunk = 4

    def eliminate(start, pair):
        base = pl.multiple_of(pair * order, order)
        col0, col1 = both(system[pl.ds(base, order), :])
        pivot0 = 2 * pair
        d0, e0 = both(system[pl.ds(base + pivot0, 1), :])
        _, f0 = both(system[pl.ds(base + pivot0 + 1, 1), :])
        inv0 = 1.0 / d0
        ratio = e0 * inv0
        inv1 = 1.0 / (f0 - ratio * e0)
        inverse[pl.ds(pivot0, 1), :] = inv0
        inverse[pl.ds(pivot0 + 1, 1), :] = inv1
        fac0 = jnp.where(level == pivot0, 0.0, col0 * inv0)
        fac1 = jnp.where(level == pivot0 + 1, 0.0, (col1 - fac0 * e0) * inv1)

        for block in list(range(start, blocks)) + [blocks]:
            at = block * order
            row0 = system[pl.ds(at + pivot0, 1), :]
            row1 = system[pl.ds(at + pivot0 + 1, 1), :] - ratio * row0
            system[at : at + order, :] = system[at : at + order, :] - fac0 * row0 - fac1 * row1

    for start in range(0, blocks, chunk):
        def step(pair, carry, start=start):
            eliminate(start, pair)
            return carry

        lax.fori_loop(start, start + chunk, step, 0)

    solved = system[blocks * order : (blocks + 1) * order, :] * inverse[...]
    sums = jnp.sum(solved, axis=0, keepdims=True)
    share = sums / pltpu.roll(sums, 64, 1)
    coef = (solved - pltpu.roll(solved, 64, 1) * share)[:, :members]
    coef = coef - jnp.mean(coef, axis=0, keepdims=True)
    names = lax.broadcasted_iota(jnp.int32, (everyone, members), 0)
    mixing = jnp.zeros((everyone, members), F32)
    for i in range(order):
        mixing = jnp.where(names == near_turned[i : i + 1, :members], coef[i : i + 1], mixing)

    sources = jnp.concatenate(
        [from_left[EDGE - HALO :, :], turned_all[...], from_right[:HALO, :]], axis=0
    )
    own = jnp.concatenate(
        [
            pick(from_left[...], group, members)[EDGE - HALO :],
            field[...].T,
            pick(from_right[...], group, members)[:HALO],
        ],
        axis=0,
    )
    ext = own + jnp.dot(
        sources, mixing, precision=lax.Precision.HIGHEST, preferred_element_type=F32
    )
    cells = field.shape[1]
    updated[...] = ext[HALO : HALO + cells].T
    surrogate(ext, space, taps1, taps2, last, columns, first, second, heads, turned)
    new_heads[...] = turned[...].T


def on_device(
    log_field, obs_heads, obs_var, obs_noise, obs_index, obs_count, neighbours,
    lift_gain, lift_bias, conv_first, bias_first, conv_second, bias_second, readout,
):
    members, cells = log_field.shape
    spaces = lax.axis_size("space")
    channels = lift_gain.shape[0]
    slots = obs_var.shape[0]
    order = neighbours.shape[1]
    everyone = lax.all_gather(log_field, "members", axis=0, tiled=True)
    total = everyone.shape[0]
    turned_all, low, high = call(
        edges_kernel,
        (shape((cells, total)), shape((EDGE, total)), shape((EDGE, total))),
        (everyone,),
    )
    forward = [(i, i + 1) for i in range(spaces - 1)]
    backward = [(i + 1, i) for i in range(spaces - 1)]
    from_left = lax.ppermute(high, "space", forward)
    from_right = lax.ppermute(low, "space", backward)
    taps1, taps2, last, columns, near, near_turned = call(
        weights_kernel,
        (
            shape((channels, 3 * channels), BF16),
            shape((channels + 16, 6 * channels), BF16),
            shape((16, channels), BF16),
            shape((4, channels, 128)),
            shape((2 * members, 2 * order), jnp.int32),
            shape((2 * order, members), jnp.int32),
        ),
        (lift_gain, lift_bias, conv_first, bias_first, conv_second, bias_second, readout, neighbours),
        scratch=(
            pltpu.VMEM((channels, 3 * channels), F32),
            pltpu.VMEM((channels + 16, 6 * channels), F32),
        ),
        flops=1 << 22,
    )
    run = cells // PARTS
    rows = run + 2 * HALO
    lanes = PARTS * members
    work = (
        pltpu.VMEM((rows, channels, lanes), BF16),
        pltpu.VMEM((rows - 2, channels, lanes), BF16),
        pltpu.VMEM((run, lanes), F32),
        pltpu.VMEM((cells, members), F32),
    )
    sent = call(
        observe_kernel,
        shape((spaces, slots, 2 * members)),
        (
            log_field, from_left, from_right, taps1, taps2, last, columns,
            obs_heads, obs_var, obs_noise, obs_index, obs_count,
        ),
        in_specs=[VMEM] * 10 + [SMEM] * 2,
        scratch=work + (pltpu.VMEM((slots, members), F32),),
    )
    got = lax.all_to_all(sent, "space", 0, 0)
    got = lax.all_gather(got, "members", axis=0, tiled=False)
    return call(
        update_kernel,
        (shape((members, cells)), shape((members, cells))),
        (
            got, log_field, turned_all, from_left, from_right,
            taps1, taps2, last, columns, near, near_turned,
        ),
        scratch=(
            pltpu.VMEM(((order // 2 + 1) * order, 128), F32),
            pltpu.VMEM((order, 128), F32),
        )
        + work,
    )


def solution(mesh):
    in_specs = (
        P("members", "space"),
        P("space"),
        P("space"),
        P("members", "space"),
        P("space", None),
        P("space"),
        P("members", None),
        P(),
        P(),
        P(),
        P(),
        P(),
        P(),
        P(),
    )
    out_specs = (P("members", "space"), P("members", "space"))
    return jax.shard_map(
        on_device, mesh=mesh, in_specs=in_specs, out_specs=out_specs, check_vma=False
    )
```

```python
import jax
import jax.numpy as jnp
from jax import lax
from jax.experimental import pallas as pl
from jax.experimental.pallas import tpu as pltpu
from jax.sharding import PartitionSpec as P

F32 = jnp.float32
BF16 = jnp.bfloat16
HALO = 3
EDGE = 8
PARTS = 4
VMEM = pl.BlockSpec(memory_space=pltpu.VMEM)
SMEM = pl.BlockSpec(memory_space=pltpu.SMEM)


def shape(dims, dtype=F32):
    return jax.ShapeDtypeStruct(dims, dtype)


def call(kernel, outs, args, in_specs=None, scratch=(), flops=0, limit=40):
    return pl.pallas_call(
        kernel,
        out_shape=outs,
        in_specs=in_specs or [VMEM] * len(args),
        out_specs=jax.tree.map(lambda _: VMEM, outs),
        scratch_shapes=list(scratch),
        cost_estimate=pl.CostEstimate(flops=flops, bytes_accessed=1 << 18, transcendentals=0),
        compiler_params=pltpu.CompilerParams(vmem_limit_bytes=limit << 20),
    )(*args)


def column(row):
    size = row.shape[1]
    same = lax.broadcasted_iota(jnp.int32, (size, size), 0) == lax.broadcasted_iota(
        jnp.int32, (size, size), 1
    )
    return jnp.sum(jnp.where(same, row, 0.0), axis=1, keepdims=True)


def edges_kernel(field, low, high):
    value = field[...].T
    low[...] = value[:EDGE]
    high[...] = value[value.shape[0] - EDGE :]


def layers(wide, run, left, right, taps1, taps2, columns, first, second, heads):
    lanes = wide.shape[1]
    rows = run + 2 * HALO
    gain, bias, bias1, bias2, last = [
        jnp.concatenate([columns[i]] * (lanes // columns.shape[2]), axis=1) for i in range(5)
    ]
    channels = gain.shape[0]
    for r in range(rows):
        value = jnp.tanh(gain * wide[r : r + 1] + bias)
        if left is not None and r < HALO:
            value = value * left
        if right is not None and r >= rows - HALO:
            value = value * right
        first[r] = value.astype(BF16)
    for i in range(rows - 2):
        window = first[i : i + 3].reshape(3 * channels, lanes)
        half = jnp.dot(taps1[...], window, preferred_element_type=F32) + bias1
        value = half + half * jnp.tanh(half)
        if left is not None and i < HALO - 1:
            value = value * left
        if right is not None and i >= rows - 2 - (HALO - 1):
            value = value * right
        second[i] = value.astype(BF16)
    split = 3 * channels
    for n in range(run):
        window1 = jnp.concatenate([first[n + 1], first[n + 3], first[n + 5]], axis=0)
        window2 = jnp.concatenate([second[n], second[n + 2], second[n + 4]], axis=0)
        total = jnp.dot(taps2[:, :split], window1, preferred_element_type=F32) + jnp.dot(
            taps2[:, split:], window2, preferred_element_type=F32
        )
        half = total[:channels] + bias2
        third = (half + half * jnp.tanh(half)).astype(BF16).astype(F32)
        rest = jnp.sum(third * last, axis=0, keepdims=True)
        heads[n : n + 1, :] = total[channels : channels + 1] + rest


def in_runs(ext):
    run = (ext.shape[0] - 2 * HALO) // PARTS
    return jnp.concatenate([ext[q * run : (q + 1) * run + 2 * HALO] for q in range(PARTS)], axis=1)


def prepare_kernel(
    field, gain, bias, conv1, bias1, conv2, bias2, readout, neighbours,
    taps1, taps2, columns, near, near_turned, own, inner,
    wide1, wide2, first, second, heads,
):
    channels = gain.shape[0]
    split = 3 * channels
    row = readout[...].astype(F32).reshape(1, split)
    wide2[...] = jnp.zeros_like(wide2)
    for tap in range(3):
        at = slice(tap * channels, (tap + 1) * channels)
        wide1[:, at] = 0.5 * conv1[tap].astype(F32)
        both = 0.5 * conv2[tap].astype(F32)
        wide2[0:channels, at] = both[:, :channels]
        wide2[0:channels, split + tap * channels : split + (tap + 1) * channels] = both[:, channels:]
    wide2[channels : channels + 1, channels : 2 * channels] = row[:, :channels]
    wide2[channels : channels + 1, split + channels : split + 2 * channels] = row[
        :, channels : 2 * channels
    ]
    taps1[...] = wide1[...].astype(BF16)
    taps2[...] = wide2[...].astype(BF16)
    rows = [
        gain[...].reshape(1, channels),
        bias[...].reshape(1, channels),
        0.5 * bias1[...].reshape(1, channels),
        0.5 * bias2[...].reshape(1, channels),
        row[:, 2 * channels :],
    ]
    for spot, value in enumerate(rows):
        columns[spot] = jnp.broadcast_to(column(value), (channels, columns.shape[2]))
    ids = neighbours[...]
    pair = jnp.concatenate([ids, ids], axis=1)
    near[...] = jnp.concatenate([pair, pair], axis=0)
    near_turned[...] = pair.T
    turned = field[...].T
    own[...] = turned
    members = turned.shape[1]
    zeros = jnp.zeros((HALO, members), F32)
    wide = in_runs(jnp.concatenate([zeros, turned, zeros], axis=0))
    run = turned.shape[0] // PARTS
    layers(wide, run, None, None, taps1, taps2, columns, first, second, heads)
    for q in range(PARTS):
        inner[q * run : (q + 1) * run, :] = heads[:, q * members : (q + 1) * members]


def observe_kernel(
    own, inner, from_left, from_right, taps1, taps2, columns,
    obs_heads, obs_var, obs_noise, obs_index, obs_count,
    sent, ext, first, second, heads, turned, chosen,
):
    space = lax.axis_index("space")
    spaces = lax.axis_size("space")
    cells, members = own.shape
    ext[0:EDGE, :] = from_left[...]
    ext[EDGE : EDGE + cells, :] = own[...]
    ext[EDGE + cells :, :] = from_right[...]
    ends = jnp.concatenate(
        [ext[EDGE - HALO : EDGE + 2 * HALO, :], ext[EDGE + cells - 2 * HALO : EDGE + cells + HALO, :]],
        axis=1,
    )
    lane = lax.broadcasted_iota(jnp.int32, (1, 2 * members), 1)
    left = jnp.where((lane < members) & (space == 0), 0.0, 1.0)
    right = jnp.where((lane >= members) & (space == spaces - 1), 0.0, 1.0)
    layers(ends, HALO, left, right, taps1, taps2, columns, first, second, heads)
    turned[...] = inner[...]
    turned[0:HALO, :] = heads[0:HALO, :members]
    turned[cells - HALO :, :] = heads[0:HALO, members:]
    slots = obs_var.shape[0]
    for k in range(slots):
        chosen[k : k + 1, :] = turned[pl.ds(obs_index[0, k], 1), :]
    own_obs = chosen[...]
    target = column(obs_heads[...].reshape(1, slots))
    variance = column(obs_var[...].reshape(1, slots))
    live = lax.broadcasted_iota(jnp.int32, (slots, 1), 0) < obs_count[0]
    root = jnp.where(live, lax.rsqrt(variance), 0.0)
    innovation = target + jnp.sqrt(variance) * obs_noise[...].T - own_obs
    payload = jnp.concatenate([root * own_obs, root * innovation], axis=1)
    for copy in range(sent.shape[0]):
        sent[copy] = payload


def split3(value):
    one = value.astype(BF16)
    rest = value - one.astype(F32)
    two = rest.astype(BF16)
    three = (rest - two.astype(F32)).astype(BF16)
    return jnp.concatenate([one, two, three], axis=1)


def lane_gather(table, index):
    low = index & 127
    high = index >> 7
    found = None
    for tile in range(table.shape[1] // 128):
        part = jnp.take_along_axis(
            table[:, tile * 128 : (tile + 1) * 128], low, axis=1, mode="promise_in_bounds"
        )
        found = part if found is None else jnp.where(high == tile, part, found)
    return found


def update_kernel(
    got, ext, taps1, taps2, columns, near, near_turned,
    updated, new_heads,
    system, first, second, heads, turned,
):
    space = lax.axis_index("space")
    spaces = lax.axis_size("space")
    group = lax.axis_index("members")
    groups, slots = got.shape[0], got.shape[1] * got.shape[2]
    members = got.shape[3] // 2
    everyone = groups * members
    order = near.shape[0] // 2
    half_lane = lax.broadcasted_iota(jnp.int32, (1, 128), 1) < 64

    panel = jnp.concatenate(
        [got[g].reshape(slots, 2 * members)[:, :members] for g in range(groups)], axis=1
    )
    panel = panel - jnp.mean(panel, axis=1, keepdims=True)
    innovation = got[group].reshape(slots, 2 * members)[:, members:]
    stacked = jnp.concatenate([panel, innovation], axis=1)
    product = lax.dot_general(
        stacked, panel, (((0,), (0,)), ((), ())),
        precision=lax.Precision.HIGHEST, preferred_element_type=F32,
    )
    gram = split3(product[:everyone])
    sides = product[everyone:]

    ids = near[...]
    second_half = (lax.broadcasted_iota(jnp.int32, (128, 128), 0) >= 64).astype(jnp.int32)
    lane_id = lax.broadcasted_iota(jnp.int32, (128, 128), 1)
    row_id = lax.broadcasted_iota(jnp.int32, (128, 128), 0)
    everyone_id = lax.broadcasted_iota(jnp.int32, (128, everyone), 1)

    def extract(quad, carry):
        found = []
        for b in range(2):
            column_id = 4 * quad + 2 * b + second_half
            member = jnp.take_along_axis(ids, column_id, axis=1, mode="promise_in_bounds")
            member = jnp.concatenate([member] * (everyone // 128), axis=1)
            chosen = jnp.where(member == everyone_id, 1.0, 0.0).astype(BF16)
            parts = jnp.dot(chosen, gram, preferred_element_type=F32)
            rows = (
                parts[:, :everyone]
                + parts[:, everyone : 2 * everyone]
                + parts[:, 2 * everyone :]
            )
            found.append(lane_gather(rows, ids))
        block = jnp.where(half_lane, found[0], found[1]).T
        own = 4 * quad + 2 * (row_id >= 64).astype(jnp.int32) + (lane_id >= 64).astype(jnp.int32)
        block = block + jnp.where((row_id & 63) == own, order - 1.0, 0.0)
        system[pl.ds(pl.multiple_of(quad * 128, 128), 128), :] = block
        return carry

    lax.fori_loop(0, order // 4, extract, 0, unroll=order // 4)
    side = lane_gather(jnp.concatenate([sides, sides], axis=0), ids)
    side = jnp.where(row_id >= 64, 1.0, side).T[:order]
    system[order // 2 * order : (order // 2 + 1) * order, :] = side

    blocks = order // 2
    level = lax.broadcasted_iota(jnp.int32, (order, 128), 0)

    def both(value):
        turn = pltpu.roll(value, 64, 1)
        return jnp.where(half_lane, value, turn), jnp.where(half_lane, turn, value)

    def factors(current, pair):
        one, two = 2 * pair, 2 * pair + 1
        col0, col1 = both(current)
        d0, e0 = col0[one:two], col1[one:two]
        inv0 = 1.0 / d0
        ratio = e0 * inv0
        inv1 = 1.0 / (col1[two : two + 1] - ratio * e0)
        fac0 = jnp.where(level == one, 0.0, col0 * inv0)
        fac1 = jnp.where(level == two, 0.0, (col1 - fac0 * e0) * inv1)
        return fac0, fac1, ratio, inv0, inv1

    def eliminated(block, pair, fac0, fac1, ratio):
        at = block * order
        row0 = system[at + 2 * pair : at + 2 * pair + 1, :]
        row1 = system[at + 2 * pair + 1 : at + 2 * pair + 2, :] - ratio * row0
        return system[at : at + order, :] - fac0 * row0 - fac1 * row1

    inverses = []
    fac0, fac1, ratio, inv0, inv1 = factors(system[0:order, :], 0)
    for pair in range(blocks):
        inverses += [inv0, inv1]
        ahead = eliminated(pair + 1, pair, fac0, fac1, ratio)
        if pair + 1 < blocks:
            later = factors(ahead, pair + 1)
        for block in range(pair + 2, blocks + 1):
            system[block * order : (block + 1) * order, :] = eliminated(
                block, pair, fac0, fac1, ratio
            )
        if pair + 1 < blocks:
            fac0, fac1, ratio, inv0, inv1 = later
    solved = ahead * jnp.concatenate(inverses, axis=0)
    sums = jnp.sum(solved, axis=0, keepdims=True)
    share = sums / pltpu.roll(sums, 64, 1)
    coef = (solved - pltpu.roll(solved, 64, 1) * share)[:, :members]
    coef = coef - jnp.mean(coef, axis=0, keepdims=True)
    names = lax.broadcasted_iota(jnp.int32, (everyone, members), 0)
    mixing = jnp.zeros((everyone, members), F32)
    for i in range(order):
        mixing = jnp.where(names == near_turned[i : i + 1, :members], coef[i : i + 1], mixing)

    cells = updated.shape[1]
    inside = slice(EDGE - HALO, EDGE + cells + HALO)
    sources = jnp.concatenate([ext[g][inside] for g in range(groups)], axis=1)
    field = ext[group][inside] + jnp.dot(
        sources, mixing, precision=lax.Precision.HIGHEST, preferred_element_type=F32
    )
    updated[...] = field[HALO : HALO + cells].T
    run = cells // PARTS
    lane = lax.broadcasted_iota(jnp.int32, (1, PARTS * members), 1)
    left = jnp.where((lane < members) & (space == 0), 0.0, 1.0)
    right = jnp.where((lane >= (PARTS - 1) * members) & (space == spaces - 1), 0.0, 1.0)
    layers(in_runs(field), run, left, right, taps1, taps2, columns, first, second, heads)
    for q in range(PARTS):
        turned[q * run : (q + 1) * run, :] = heads[:, q * members : (q + 1) * members]
    new_heads[...] = turned[...].T


def on_device(
    log_field, obs_heads, obs_var, obs_noise, obs_index, obs_count, neighbours,
    lift_gain, lift_bias, conv_first, bias_first, conv_second, bias_second, readout,
):
    members, cells = log_field.shape
    spaces = lax.axis_size("space")
    channels = lift_gain.shape[0]
    slots = obs_var.shape[0]
    order = neighbours.shape[1]
    low, high = call(
        edges_kernel, (shape((EDGE, members)), shape((EDGE, members))), (log_field,)
    )
    forward = [(i, i + 1) for i in range(spaces - 1)]
    backward = [(i + 1, i) for i in range(spaces - 1)]
    from_left = lax.ppermute(high, "space", forward)
    from_right = lax.ppermute(low, "space", backward)

    def work(run, parts):
        rows, lanes = run + 2 * HALO, parts * members
        return (
            pltpu.VMEM((rows, channels, lanes), BF16),
            pltpu.VMEM((rows - 2, channels, lanes), BF16),
            pltpu.VMEM((max(run, 8), lanes), F32),
        )

    taps1, taps2, columns, near, near_turned, own, inner = call(
        prepare_kernel,
        (
            shape((channels, 3 * channels), BF16),
            shape((channels + 16, 6 * channels), BF16),
            shape((5, channels, 128)),
            shape((2 * members, 2 * order), jnp.int32),
            shape((2 * order, members), jnp.int32),
            shape((cells, members)),
            shape((cells, members)),
        ),
        (
            log_field, lift_gain, lift_bias, conv_first, bias_first, conv_second, bias_second,
            readout, neighbours,
        ),
        scratch=(
            pltpu.VMEM((channels, 3 * channels), F32),
            pltpu.VMEM((channels + 16, 6 * channels), F32),
        )
        + work(cells // PARTS, PARTS),
        flops=1 << 29,
    )
    sent, ext = call(
        observe_kernel,
        (shape((spaces, slots, 2 * members)), shape((2 * EDGE + cells, members))),
        (
            own, inner, from_left, from_right, taps1, taps2, columns,
            obs_heads, obs_var, obs_noise, obs_index, obs_count,
        ),
        in_specs=[VMEM] * 10 + [SMEM] * 2,
        scratch=work(HALO, 2)
        + (pltpu.VMEM((cells, members), F32), pltpu.VMEM((slots, members), F32)),
    )
    got = lax.all_to_all(sent, "space", 0, 0)
    got, ext = lax.all_gather((got, ext), "members", axis=0, tiled=False)
    return call(
        update_kernel,
        (shape((members, cells)), shape((members, cells))),
        (got, ext, taps1, taps2, columns, near, near_turned),
        scratch=(pltpu.VMEM(((order // 2 + 1) * order, 128), F32),)
        + work(cells // PARTS, PARTS)
        + (pltpu.VMEM((cells, members), F32),),
    )


def solution(mesh):
    in_specs = (
        P("members", "space"),
        P("space"),
        P("space"),
        P("members", "space"),
        P("space", None),
        P("space"),
        P("members", None),
        P(),
        P(),
        P(),
        P(),
        P(),
        P(),
        P(),
    )
    out_specs = (P("members", "space"), P("members", "space"))
    return jax.shard_map(
        on_device, mesh=mesh, in_specs=in_specs, out_specs=out_specs, check_vma=False
    )
```

```python
import functools

import jax
import jax.numpy as jnp
from jax import lax
from jax.experimental import pallas as pl
from jax.experimental.pallas import tpu as pltpu
from jax.sharding import PartitionSpec as P

F32 = jnp.float32
BF16 = jnp.bfloat16
HALO = 3
EDGE = 8
PARTS = 4
VMEM = pl.BlockSpec(memory_space=pltpu.VMEM)


def shape(dims, dtype=F32):
    return jax.ShapeDtypeStruct(dims, dtype)


def call(kernel, outs, args, scratch=(), flops=0, limit=40):
    return pl.pallas_call(
        kernel,
        out_shape=outs,
        in_specs=[VMEM] * len(args),
        out_specs=jax.tree.map(lambda _: VMEM, outs),
        scratch_shapes=list(scratch),
        cost_estimate=pl.CostEstimate(flops=flops, bytes_accessed=1 << 18, transcendentals=0),
        compiler_params=pltpu.CompilerParams(vmem_limit_bytes=limit << 20),
    )(*args)


def column(row):
    size = row.shape[1]
    same = lax.broadcasted_iota(jnp.int32, (size, size), 0) == lax.broadcasted_iota(
        jnp.int32, (size, size), 1
    )
    return jnp.sum(jnp.where(same, row, 0.0), axis=1, keepdims=True)


def layers(wide, run, left, right, taps1, taps2, columns, first, second, heads):
    lanes = wide.shape[1]
    rows = run + 2 * HALO
    gain, bias, bias1, bias2, last = [
        jnp.concatenate([columns[i]] * (lanes // columns.shape[2]), axis=1) for i in range(5)
    ]
    channels = gain.shape[0]
    for r in range(rows):
        value = jnp.tanh(gain * wide[r : r + 1] + bias)
        if left is not None and r < HALO:
            value = value * left
        if right is not None and r >= rows - HALO:
            value = value * right
        first[r] = value.astype(BF16)
    for i in range(rows - 2):
        window = first[i : i + 3].reshape(3 * channels, lanes)
        half = jnp.dot(taps1[...], window, preferred_element_type=F32) + bias1
        value = half + half * jnp.tanh(half)
        if left is not None and i < HALO - 1:
            value = value * left
        if right is not None and i >= rows - 2 - (HALO - 1):
            value = value * right
        second[i] = value.astype(BF16)
    split = 3 * channels
    for n in range(run):
        window1 = jnp.concatenate([first[n + 1], first[n + 3], first[n + 5]], axis=0)
        window2 = jnp.concatenate([second[n], second[n + 2], second[n + 4]], axis=0)
        total = jnp.dot(taps2[:, :split], window1, preferred_element_type=F32) + jnp.dot(
            taps2[:, split:], window2, preferred_element_type=F32
        )
        half = total[:channels] + bias2
        third = (half + half * jnp.tanh(half)).astype(BF16).astype(F32)
        rest = jnp.sum(third * last, axis=0, keepdims=True)
        heads[n : n + 1, :] = total[channels : channels + 1] + rest


def in_runs(ext):
    run = (ext.shape[0] - 2 * HALO) // PARTS
    return jnp.concatenate([ext[q * run : (q + 1) * run + 2 * HALO] for q in range(PARTS)], axis=1)


def split3(value):
    one = value.astype(BF16)
    rest = value - one.astype(F32)
    two = rest.astype(BF16)
    three = (rest - two.astype(F32)).astype(BF16)
    return jnp.concatenate([one, two, three], axis=1)


def edges_kernel(field, low, high, own):
    turned = field[...].T
    cells = turned.shape[0]
    own[...] = turned
    low[...] = turned[:EDGE]
    high[...] = turned[cells - EDGE :]


def prepare_kernel(
    own, gain, bias, conv1, bias1, conv2, bias2, readout, neighbours,
    obs_heads, obs_var, noise_turned, obs_index, obs_count,
    taps1, taps2, columns, near, near_turned, chosen, goal, inner,
    wide1, wide2, first, second, heads,
):
    turned = own[...]
    cells, members = turned.shape
    channels = gain.shape[0]
    split = 3 * channels
    row = readout[...].astype(F32).reshape(1, split)
    wide2[...] = jnp.zeros_like(wide2)
    for tap in range(3):
        at = slice(tap * channels, (tap + 1) * channels)
        wide1[:, at] = 0.5 * conv1[tap].astype(F32)
        both = 0.5 * conv2[tap].astype(F32)
        wide2[0:channels, at] = both[:, :channels]
        wide2[0:channels, split + tap * channels : split + (tap + 1) * channels] = both[:, channels:]
    wide2[channels : channels + 1, channels : 2 * channels] = row[:, :channels]
    wide2[channels : channels + 1, split + channels : split + 2 * channels] = row[
        :, channels : 2 * channels
    ]
    taps1[...] = wide1[...].astype(BF16)
    taps2[...] = wide2[...].astype(BF16)
    rows = [
        gain[...].reshape(1, channels),
        bias[...].reshape(1, channels),
        0.5 * bias1[...].reshape(1, channels),
        0.5 * bias2[...].reshape(1, channels),
        row[:, 2 * channels :],
    ]
    for spot, value in enumerate(rows):
        columns[spot] = jnp.broadcast_to(column(value), (channels, columns.shape[2]))
    everyone = members * lax.axis_size("members")
    ids = neighbours[...] - members * lax.axis_index("members")
    ids = jnp.where(ids < 0, ids + everyone, ids)
    pair = jnp.concatenate([ids, ids], axis=1)
    near[...] = jnp.concatenate([pair, pair], axis=0)
    near_turned[...] = pair.T
    slots = obs_var.shape[0]
    cell = column(obs_index[...].astype(F32)).astype(jnp.int32)
    chosen[...] = jnp.where(
        lax.broadcasted_iota(jnp.int32, (slots, cells), 1) == cell, 1.0, 0.0
    ).astype(BF16)
    target = column(obs_heads[...].reshape(1, slots))
    variance = column(obs_var[...].reshape(1, slots))
    live = lax.broadcasted_iota(jnp.int32, (slots, 1), 0) < obs_count[...].reshape(1, 1)
    root = jnp.where(live, lax.rsqrt(variance), 0.0)
    wanted = root * (target + jnp.sqrt(variance) * noise_turned[...])
    goal[...] = jnp.concatenate([jnp.broadcast_to(root, (slots, members)), wanted], axis=1)
    zeros = jnp.zeros((HALO, members), F32)
    wide = in_runs(jnp.concatenate([zeros, turned, zeros], axis=0))
    run = cells // PARTS
    layers(wide, run, None, None, taps1, taps2, columns, first, second, heads)
    for q in range(PARTS):
        inner[q * run : (q + 1) * run, :] = heads[:, q * members : (q + 1) * members]


def observe_kernel(
    own, inner, from_left, from_right, taps1, taps2, columns, chosen, goal,
    sent, ext, first, second, heads,
):
    space = lax.axis_index("space")
    spaces = lax.axis_size("space")
    cells, members = own.shape
    ext[0:EDGE, :] = from_left[...]
    ext[EDGE : EDGE + cells, :] = own[...]
    ext[EDGE + cells :, :] = from_right[...]
    ends = jnp.concatenate(
        [
            jnp.concatenate([from_left[EDGE - HALO :, :], own[0 : 2 * HALO, :]], axis=0),
            jnp.concatenate([own[cells - 2 * HALO :, :], from_right[0:HALO, :]], axis=0),
        ],
        axis=1,
    )
    lane = lax.broadcasted_iota(jnp.int32, (1, 2 * members), 1)
    left = jnp.where((lane < members) & (space == 0), 0.0, 1.0)
    right = jnp.where((lane >= members) & (space == spaces - 1), 0.0, 1.0)
    layers(ends, HALO, left, right, taps1, taps2, columns, first, second, heads)
    every = jnp.concatenate(
        [heads[0:HALO, :members], inner[HALO : cells - HALO, :], heads[0:HALO, members:]], axis=0
    )
    parts = jnp.dot(chosen[...], split3(every), preferred_element_type=F32)
    seen = parts[:, :members] + parts[:, members : 2 * members] + parts[:, 2 * members :]
    weighted = goal[:, :members] * seen
    payload = jnp.concatenate([weighted, goal[:, members:] - weighted], axis=1)
    for copy in range(sent.shape[0]):
        sent[copy] = payload


def lane_gather(table, index):
    low = index & 127
    high = index >> 7
    found = None
    for tile in range(table.shape[1] // 128):
        part = jnp.take_along_axis(
            table[:, tile * 128 : (tile + 1) * 128], low, axis=1, mode="promise_in_bounds"
        )
        found = part if found is None else jnp.where(high == tile, part, found)
    return found


def update_kernel(groups, *refs):
    gots, exts = refs[:groups], refs[groups : 2 * groups]
    (
        taps1, taps2, columns, near, near_turned,
        updated, new_heads,
        system, first, second, heads, turned,
    ) = refs[2 * groups :]
    space = lax.axis_index("space")
    spaces = lax.axis_size("space")
    slots = gots[0].shape[0] * gots[0].shape[1]
    members = gots[0].shape[2] // 2
    everyone = groups * members
    order = near.shape[0] // 2
    half_lane = lax.broadcasted_iota(jnp.int32, (1, 128), 1) < 64

    whole = [got[...].reshape(slots, 2 * members) for got in gots]
    panel = jnp.concatenate([rows[:, :members] for rows in whole], axis=1)
    panel = panel - jnp.mean(panel, axis=1, keepdims=True)
    innovation = whole[0][:, members:]
    stacked = jnp.concatenate([panel, innovation], axis=1)
    product = lax.dot_general(
        stacked, panel, (((0,), (0,)), ((), ())),
        precision=lax.Precision.HIGHEST, preferred_element_type=F32,
    )
    gram = split3(product[:everyone])
    sides = product[everyone:]

    ids = near[...]
    second_half = (lax.broadcasted_iota(jnp.int32, (128, 128), 0) >= 64).astype(jnp.int32)
    lane_id = lax.broadcasted_iota(jnp.int32, (128, 128), 1)
    row_id = lax.broadcasted_iota(jnp.int32, (128, 128), 0)
    everyone_id = lax.broadcasted_iota(jnp.int32, (128, everyone), 1)

    def extract(quad, carry):
        found = []
        for b in range(2):
            column_id = 4 * quad + 2 * b + second_half
            member = jnp.take_along_axis(ids, column_id, axis=1, mode="promise_in_bounds")
            member = jnp.concatenate([member] * (everyone // 128), axis=1)
            chosen = jnp.where(member == everyone_id, 1.0, 0.0).astype(BF16)
            parts = jnp.dot(chosen, gram, preferred_element_type=F32)
            rows = (
                parts[:, :everyone]
                + parts[:, everyone : 2 * everyone]
                + parts[:, 2 * everyone :]
            )
            found.append(lane_gather(rows, ids))
        block = jnp.where(half_lane, found[0], found[1]).T
        own = 4 * quad + 2 * (row_id >= 64).astype(jnp.int32) + (lane_id >= 64).astype(jnp.int32)
        block = block + jnp.where((row_id & 63) == own, order - 1.0, 0.0)
        system[pl.ds(pl.multiple_of(quad * 128, 128), 128), :] = block
        return carry

    lax.fori_loop(0, order // 4, extract, 0, unroll=order // 4)
    side = lane_gather(jnp.concatenate([sides, sides], axis=0), ids)
    side = jnp.where(row_id >= 64, 1.0, side).T[:order]
    system[order // 2 * order : (order // 2 + 1) * order, :] = side

    blocks = order // 2
    def both(value):
        turn = pltpu.roll(value, 64, 1)
        return jnp.where(half_lane, value, turn), jnp.where(half_lane, turn, value)

    def without(value, pair):
        at = 2 * pair // 8 * 8
        row = lax.broadcasted_iota(jnp.int32, (8, 128), 0) + at
        tile = jnp.where((row >= 2 * pair) & (row < 2 * pair + 2), 0.0, value[at : at + 8])
        parts = [value[:at], tile, value[at + 8 :]]
        return jnp.concatenate([part for part in parts if part.shape[0]], axis=0)

    def factors(col0, col1, pair):
        one, two = 2 * pair, 2 * pair + 1
        d, e, f = col0[one:two], col1[one:two], col1[two : two + 1]
        inv = 1.0 / (d * f - e * e)
        fac0 = without((col0 * f - col1 * e) * inv, pair)
        fac1 = without((col1 * d - col0 * e) * inv, pair)
        return fac0, fac1, (f * inv, d * inv, e * inv)

    own_share, cross_share = [], []
    fac0, fac1, shares = factors(*both(system[0:order, :]), 0)
    for pair in range(blocks):
        own_share += [shares[0], shares[1]]
        cross_share += [shares[2], shares[2]]
        one, two = 2 * pair, 2 * pair + 1
        if pair + 1 < blocks:
            col0, col1 = both(system[(pair + 1) * order : (pair + 2) * order, :])
            later = factors(
                col0 - fac0 * col0[one:two] - fac1 * col0[two : two + 1],
                col1 - fac0 * col1[one:two] - fac1 * col1[two : two + 1],
                pair + 1,
            )
        for block in range(min(pair + 2, blocks), blocks + 1):
            at = block * order
            row0 = system[at + one : at + two, :]
            row1 = system[at + two : at + two + 1, :]
            system[at : at + order, :] = system[at : at + order, :] - fac0 * row0 - fac1 * row1
        if pair + 1 < blocks:
            fac0, fac1, shares = later
    sides = system[blocks * order :, :]
    even = lax.broadcasted_iota(jnp.int32, (order, 128), 0) % 2 == 0
    partner = jnp.where(even, pltpu.roll(sides, order - 1, 0), pltpu.roll(sides, 1, 0))
    solved = sides * jnp.concatenate(own_share, axis=0) - partner * jnp.concatenate(
        cross_share, axis=0
    )
    sums = jnp.sum(solved, axis=0, keepdims=True)
    share = sums / pltpu.roll(sums, 64, 1)
    coef = (solved - pltpu.roll(solved, 64, 1) * share)[:, :members]
    coef = coef - jnp.mean(coef, axis=0, keepdims=True)
    names = lax.broadcasted_iota(jnp.int32, (everyone, members), 0)
    mixing = jnp.zeros((everyone, members), F32)
    for i in range(order):
        mixing = jnp.where(names == near_turned[i : i + 1, :members], coef[i : i + 1], mixing)

    cells = updated.shape[1]
    inside = slice(EDGE - HALO, EDGE + cells + HALO)
    sources = jnp.concatenate([ext[inside, :] for ext in exts], axis=1)
    field = exts[0][inside, :] + jnp.dot(
        sources, mixing, precision=lax.Precision.HIGHEST, preferred_element_type=F32
    )
    updated[...] = field[HALO : HALO + cells].T
    run = cells // PARTS
    lane = lax.broadcasted_iota(jnp.int32, (1, PARTS * members), 1)
    left = jnp.where((lane < members) & (space == 0), 0.0, 1.0)
    right = jnp.where((lane >= (PARTS - 1) * members) & (space == spaces - 1), 0.0, 1.0)
    layers(in_runs(field), run, left, right, taps1, taps2, columns, first, second, heads)
    for q in range(PARTS):
        turned[q * run : (q + 1) * run, :] = heads[:, q * members : (q + 1) * members]
    new_heads[...] = turned[...].T


def from_groups(value):
    groups = lax.axis_size("members")
    found = [value]
    for step in range(1, groups):
        pairs = [((i + step) % groups, i) for i in range(groups)]
        found.append(lax.ppermute(value, "members", pairs))
    return found


def on_device(
    log_field, obs_heads, obs_var, obs_noise, obs_index, obs_count, neighbours,
    lift_gain, lift_bias, conv_first, bias_first, conv_second, bias_second, readout,
):
    members, cells = log_field.shape
    spaces = lax.axis_size("space")
    groups = lax.axis_size("members")
    channels = lift_gain.shape[0]
    slots = obs_var.shape[0]
    order = neighbours.shape[1]

    def work(run, parts):
        rows, lanes = run + 2 * HALO, parts * members
        return (
            pltpu.VMEM((rows, channels, lanes), BF16),
            pltpu.VMEM((rows - 2, channels, lanes), BF16),
            pltpu.VMEM((max(run, 8), lanes), F32),
        )

    low, high, own = call(
        edges_kernel,
        (shape((EDGE, members)), shape((EDGE, members)), shape((cells, members))),
        (log_field,),
        flops=1 << 34,
    )
    forward = [(i, i + 1) for i in range(spaces - 1)]
    backward = [(i + 1, i) for i in range(spaces - 1)]
    from_left = lax.ppermute(high, "space", forward)
    from_right = lax.ppermute(low, "space", backward)
    taps1, taps2, columns, near, near_turned, chosen, goal, inner = call(
        prepare_kernel,
        (
            shape((channels, 3 * channels), BF16),
            shape((channels + 16, 6 * channels), BF16),
            shape((5, channels, 128)),
            shape((2 * members, 2 * order), jnp.int32),
            shape((2 * order, members), jnp.int32),
            shape((slots, cells), BF16),
            shape((slots, 2 * members)),
            shape((cells, members)),
        ),
        (
            own, lift_gain, lift_bias, conv_first, bias_first, conv_second, bias_second,
            readout, neighbours, obs_heads, obs_var, obs_noise.T, obs_index, obs_count,
        ),
        scratch=(
            pltpu.VMEM((channels, 3 * channels), F32),
            pltpu.VMEM((channels + 16, 6 * channels), F32),
        )
        + work(cells // PARTS, PARTS),
        flops=1 << 29,
    )
    sent, ext = call(
        observe_kernel,
        (shape((spaces, slots, 2 * members)), shape((2 * EDGE + cells, members))),
        (own, inner, from_left, from_right, taps1, taps2, columns, chosen, goal),
        scratch=work(HALO, 2),
    )
    got = lax.all_to_all(sent, "space", 0, 0)
    return call(
        functools.partial(update_kernel, groups),
        (shape((members, cells)), shape((members, cells))),
        (*from_groups(got), *from_groups(ext), taps1, taps2, columns, near, near_turned),
        scratch=(pltpu.VMEM(((order // 2 + 1) * order, 128), F32),)
        + work(cells // PARTS, PARTS)
        + (pltpu.VMEM((cells, members), F32),),
    )


def solution(mesh):
    in_specs = (
        P("members", "space"),
        P("space"),
        P("space"),
        P("members", "space"),
        P("space", None),
        P("space"),
        P("members", None),
        P(),
        P(),
        P(),
        P(),
        P(),
        P(),
        P(),
    )
    out_specs = (P("members", "space"), P("members", "space"))
    return jax.shard_map(
        on_device, mesh=mesh, in_specs=in_specs, out_specs=out_specs, check_vma=False
    )
```

```python
import functools

import jax
import jax.numpy as jnp
from jax import lax
from jax.experimental import pallas as pl
from jax.experimental.pallas import tpu as pltpu
from jax.sharding import PartitionSpec as P

F32 = jnp.float32
BF16 = jnp.bfloat16
HALO = 3
EDGE = 8
PARTS = 4
VMEM = pl.BlockSpec(memory_space=pltpu.VMEM)


def shape(dims, dtype=F32):
    return jax.ShapeDtypeStruct(dims, dtype)


def call(kernel, outs, args, scratch=(), flops=0, limit=40):
    return pl.pallas_call(
        kernel,
        out_shape=outs,
        in_specs=[VMEM] * len(args),
        out_specs=jax.tree.map(lambda _: VMEM, outs),
        scratch_shapes=list(scratch),
        cost_estimate=pl.CostEstimate(flops=flops, bytes_accessed=1 << 18, transcendentals=0),
        compiler_params=pltpu.CompilerParams(vmem_limit_bytes=limit << 20),
    )(*args)


def column(row):
    size = row.shape[1]
    same = lax.broadcasted_iota(jnp.int32, (size, size), 0) == lax.broadcasted_iota(
        jnp.int32, (size, size), 1
    )
    return jnp.sum(jnp.where(same, row, 0.0), axis=1, keepdims=True)


def layers(wide, run, left, right, taps1, taps2, columns, first, second, heads):
    lanes = wide.shape[1]
    rows = run + 2 * HALO
    gain, bias, bias1, bias2, last = [
        jnp.concatenate([columns[i]] * (lanes // columns.shape[2]), axis=1) for i in range(5)
    ]
    channels = gain.shape[0]
    for r in range(rows):
        value = jnp.tanh(gain * wide[r : r + 1] + bias)
        if left is not None and r < HALO:
            value = value * left
        if right is not None and r >= rows - HALO:
            value = value * right
        first[r] = value.astype(BF16)
    for i in range(rows - 2):
        window = first[i : i + 3].reshape(3 * channels, lanes)
        half = jnp.dot(taps1[...], window, preferred_element_type=F32) + bias1
        value = half + half * jnp.tanh(half)
        if left is not None and i < HALO - 1:
            value = value * left
        if right is not None and i >= rows - 2 - (HALO - 1):
            value = value * right
        second[i] = value.astype(BF16)
    split = 3 * channels
    for n in range(run):
        window1 = jnp.concatenate([first[n + 1], first[n + 3], first[n + 5]], axis=0)
        window2 = jnp.concatenate([second[n], second[n + 2], second[n + 4]], axis=0)
        total = jnp.dot(taps2[:, :split], window1, preferred_element_type=F32) + jnp.dot(
            taps2[:, split:], window2, preferred_element_type=F32
        )
        half = total[:channels] + bias2
        third = (half + half * jnp.tanh(half)).astype(BF16).astype(F32)
        rest = jnp.sum(third * last, axis=0, keepdims=True)
        heads[n : n + 1, :] = total[channels : channels + 1] + rest


def in_runs(ext):
    run = (ext.shape[0] - 2 * HALO) // PARTS
    return jnp.concatenate([ext[q * run : (q + 1) * run + 2 * HALO] for q in range(PARTS)], axis=1)


def split3(value):
    one = value.astype(BF16)
    rest = value - one.astype(F32)
    two = rest.astype(BF16)
    three = (rest - two.astype(F32)).astype(BF16)
    return jnp.concatenate([one, two, three], axis=1)


def turn_kernel(field, own):
    own[...] = field[...].T


def end_masks(parts, members):
    space = lax.axis_index("space")
    lane = lax.broadcasted_iota(jnp.int32, (1, parts * members), 1)
    left = (lane < members) & (space == 0)
    right = (lane >= (parts - 1) * members) & (space == lax.axis_size("space") - 1)
    return jnp.where(left, 0.0, 1.0), jnp.where(right, 0.0, 1.0)


def prepare_kernel(
    own, gain, bias, conv1, bias1, conv2, bias2, readout, neighbours,
    obs_heads, obs_var, noise_turned, obs_index, obs_count,
    taps1, taps2, columns, near, near_turned, sent,
    wide1, wide2, first, second, heads,
):
    space = lax.axis_index("space")
    spaces = lax.axis_size("space")
    turned = own[...]
    cells, members = turned.shape
    channels = gain.shape[0]
    split = 3 * channels
    row = readout[...].astype(F32).reshape(1, split)
    wide2[...] = jnp.zeros_like(wide2)
    for tap in range(3):
        at = slice(tap * channels, (tap + 1) * channels)
        wide1[:, at] = 0.5 * conv1[tap].astype(F32)
        both = 0.5 * conv2[tap].astype(F32)
        wide2[0:channels, at] = both[:, :channels]
        wide2[0:channels, split + tap * channels : split + (tap + 1) * channels] = both[:, channels:]
    wide2[channels : channels + 1, channels : 2 * channels] = row[:, :channels]
    wide2[channels : channels + 1, split + channels : split + 2 * channels] = row[
        :, channels : 2 * channels
    ]
    taps1[...] = wide1[...].astype(BF16)
    taps2[...] = wide2[...].astype(BF16)
    rows = [
        gain[...].reshape(1, channels),
        bias[...].reshape(1, channels),
        0.5 * bias1[...].reshape(1, channels),
        0.5 * bias2[...].reshape(1, channels),
        row[:, 2 * channels :],
    ]
    for spot, value in enumerate(rows):
        columns[spot] = jnp.broadcast_to(column(value), (channels, columns.shape[2]))
    everyone = members * lax.axis_size("members")
    ids = neighbours[...] - members * lax.axis_index("members")
    ids = jnp.where(ids < 0, ids + everyone, ids)
    pair = jnp.concatenate([ids, ids], axis=1)
    near[...] = jnp.concatenate([pair, pair], axis=0)
    near_turned[...] = pair.T
    slots = obs_var.shape[0]
    cell = obs_index[...]
    low_end = (cell < HALO) & (space > 0)
    high_end = (cell >= cells - HALO) & (space < spaces - 1)
    end_row = jnp.where(
        low_end,
        (space - 1) * EDGE + HALO + cell,
        jnp.where(high_end, space * EDGE + cell - (cells - HALO), -1),
    )
    inside = column(jnp.where(end_row < 0, cell, -1).astype(F32)).astype(jnp.int32)
    chosen = jnp.where(
        lax.broadcasted_iota(jnp.int32, (slots, cells), 1) == inside, 1.0, 0.0
    ).astype(BF16)
    variance = obs_var[...].reshape(1, slots)
    live = lax.broadcasted_iota(jnp.int32, (1, slots), 1) < obs_count[...].reshape(1, 1)
    root_row = jnp.where(live, lax.rsqrt(variance), 0.0)
    root = column(root_row)
    target = column(obs_heads[...].reshape(1, slots))
    wanted = root * (target + jnp.sqrt(column(variance)) * noise_turned[...])

    zeros = jnp.zeros((HALO, members), F32)
    wide = in_runs(jnp.concatenate([zeros, turned, zeros], axis=0))
    left, right = end_masks(PARTS, members)
    layers(wide, cells // PARTS, left, right, taps1, taps2, columns, first, second, heads)
    every = jnp.concatenate(
        [heads[:, q * members : (q + 1) * members] for q in range(PARTS)], axis=0
    )
    parts = jnp.dot(chosen, split3(every), preferred_element_type=F32)
    seen = parts[:, :members] + parts[:, members : 2 * members] + parts[:, 2 * members :]
    weighted = root * seen
    blank = jnp.zeros((1, 2 * members - slots), F32)
    payload = jnp.concatenate(
        [
            jnp.concatenate([weighted, wanted - weighted], axis=1),
            jnp.concatenate([turned[: 2 * HALO], turned[cells - 2 * HALO :]], axis=1),
            jnp.concatenate([end_row.astype(F32), blank], axis=1),
            jnp.concatenate([root_row, blank], axis=1),
        ],
        axis=0,
    )
    for copy in range(sent.shape[0]):
        sent[copy] = payload


def ends_kernel(got, taps1, taps2, columns, full, first, second, heads, ends, marks):
    space = lax.axis_index("space")
    spaces = got.shape[0]
    slots = got.shape[1] - EDGE
    members = got.shape[2] // 2
    inner = 2 * HALO
    for start in range(0, spaces, PARTS):
        sides = []
        for here in range(start, start + PARTS):
            there = (here + 1) % spaces
            near_end = got[here, slots : slots + inner, members:]
            far_end = got[there, slots : slots + inner, :members]
            sides.append(jnp.concatenate([near_end, far_end], axis=0))
        wide = jnp.concatenate(sides, axis=1)
        layers(wide, inner, None, None, taps1, taps2, columns, first, second, heads)
        for q in range(PARTS):
            at = (start + q) * EDGE
            ends[at : at + EDGE, :] = heads[:, q * members : (q + 1) * members]
    for tile in range(spaces):
        at = tile * slots
        marks[0:2, at : at + slots] = got[tile, slots + inner : slots + EDGE, :slots]
    row = lax.broadcasted_iota(jnp.int32, (spaces * EDGE, spaces * slots), 0).astype(F32)
    picks = jnp.where(row == marks[0:1, :], marks[1:2, :], 0.0)
    added = lax.dot_general(
        picks, ends[...], (((0,), (0,)), ((), ())),
        precision=lax.Precision.HIGHEST, preferred_element_type=F32,
    )
    signed = jnp.concatenate([added, -added], axis=1)
    for tile in range(spaces):
        at = tile * slots
        full[at : at + slots, :] = got[tile, :slots, :] + signed[at : at + slots]
    before = jnp.where(space == 0, spaces - 1, space - 1)
    after = jnp.where(space == spaces - 1, 0, space + 1)
    at = spaces * slots
    full[at : at + EDGE, :] = got[before, slots:, :]
    full[at + EDGE : at + 2 * EDGE, :] = got[after, slots:, :]


def lane_gather(table, index):
    low = index & 127
    high = index >> 7
    found = None
    for tile in range(table.shape[1] // 128):
        part = jnp.take_along_axis(
            table[:, tile * 128 : (tile + 1) * 128], low, axis=1, mode="promise_in_bounds"
        )
        found = part if found is None else jnp.where(high == tile, part, found)
    return found


def update_kernel(groups, *refs):
    fulls, owns = refs[:groups], refs[groups : 2 * groups]
    (
        taps1, taps2, columns, near, near_turned,
        updated, new_heads,
        system, first, second, heads, turned,
    ) = refs[2 * groups :]
    slots = fulls[0].shape[0] - 2 * EDGE
    members = fulls[0].shape[1] // 2
    everyone = groups * members
    order = near.shape[0] // 2
    half_lane = lax.broadcasted_iota(jnp.int32, (1, 128), 1) < 64

    panel = jnp.concatenate([full[0:slots, :members] for full in fulls], axis=1)
    panel = panel - jnp.mean(panel, axis=1, keepdims=True)
    innovation = fulls[0][0:slots, members:]
    stacked = jnp.concatenate([panel, innovation], axis=1)
    product = lax.dot_general(
        stacked, panel, (((0,), (0,)), ((), ())),
        precision=lax.Precision.HIGHEST, preferred_element_type=F32,
    )
    gram = split3(product[:everyone])
    sides = product[everyone:]

    ids = near[...]
    second_half = (lax.broadcasted_iota(jnp.int32, (128, 128), 0) >= 64).astype(jnp.int32)
    lane_id = lax.broadcasted_iota(jnp.int32, (128, 128), 1)
    row_id = lax.broadcasted_iota(jnp.int32, (128, 128), 0)
    everyone_id = lax.broadcasted_iota(jnp.int32, (128, everyone), 1)

    def extract(quad, carry):
        found = []
        for b in range(2):
            column_id = 4 * quad + 2 * b + second_half
            member = jnp.take_along_axis(ids, column_id, axis=1, mode="promise_in_bounds")
            member = jnp.concatenate([member] * (everyone // 128), axis=1)
            chosen = jnp.where(member == everyone_id, 1.0, 0.0).astype(BF16)
            parts = jnp.dot(chosen, gram, preferred_element_type=F32)
            rows = (
                parts[:, :everyone]
                + parts[:, everyone : 2 * everyone]
                + parts[:, 2 * everyone :]
            )
            found.append(lane_gather(rows, ids))
        block = jnp.where(half_lane, found[0], found[1]).T
        own = 4 * quad + 2 * (row_id >= 64).astype(jnp.int32) + (lane_id >= 64).astype(jnp.int32)
        block = block + jnp.where((row_id & 63) == own, order - 1.0, 0.0)
        system[pl.ds(pl.multiple_of(quad * 128, 128), 128), :] = block
        return carry

    lax.fori_loop(0, order // 4, extract, 0, unroll=order // 4)
    side = lane_gather(jnp.concatenate([sides, sides], axis=0), ids)
    side = jnp.where(row_id >= 64, 1.0, side).T[:order]
    system[order // 2 * order : (order // 2 + 1) * order, :] = side

    blocks = order // 2
    def both(value):
        turn = pltpu.roll(value, 64, 1)
        return jnp.where(half_lane, value, turn), jnp.where(half_lane, turn, value)

    def without(value, pair):
        at = 2 * pair // 8 * 8
        row = lax.broadcasted_iota(jnp.int32, (8, 128), 0) + at
        tile = jnp.where((row >= 2 * pair) & (row < 2 * pair + 2), 0.0, value[at : at + 8])
        parts = [value[:at], tile, value[at + 8 :]]
        return jnp.concatenate([part for part in parts if part.shape[0]], axis=0)

    def factors(col0, col1, pair):
        one, two = 2 * pair, 2 * pair + 1
        d, e, f = col0[one:two], col1[one:two], col1[two : two + 1]
        inv = 1.0 / (d * f - e * e)
        fac0 = without((col0 * f - col1 * e) * inv, pair)
        fac1 = without((col1 * d - col0 * e) * inv, pair)
        return fac0, fac1, (f * inv, d * inv, e * inv)

    own_share, cross_share = [], []
    fac0, fac1, shares = factors(*both(system[0:order, :]), 0)
    for pair in range(blocks):
        own_share += [shares[0], shares[1]]
        cross_share += [shares[2], shares[2]]
        one, two = 2 * pair, 2 * pair + 1
        if pair + 1 < blocks:
            col0, col1 = both(system[(pair + 1) * order : (pair + 2) * order, :])
            later = factors(
                col0 - fac0 * col0[one:two] - fac1 * col0[two : two + 1],
                col1 - fac0 * col1[one:two] - fac1 * col1[two : two + 1],
                pair + 1,
            )
        for block in range(min(pair + 2, blocks), blocks + 1):
            at = block * order
            row0 = system[at + one : at + two, :]
            row1 = system[at + two : at + two + 1, :]
            system[at : at + order, :] = system[at : at + order, :] - fac0 * row0 - fac1 * row1
        if pair + 1 < blocks:
            fac0, fac1, shares = later
    sides = system[blocks * order :, :]
    even = lax.broadcasted_iota(jnp.int32, (order, 128), 0) % 2 == 0
    partner = jnp.where(even, pltpu.roll(sides, order - 1, 0), pltpu.roll(sides, 1, 0))
    solved = sides * jnp.concatenate(own_share, axis=0) - partner * jnp.concatenate(
        cross_share, axis=0
    )
    sums = jnp.sum(solved, axis=0, keepdims=True)
    share = sums / pltpu.roll(sums, 64, 1)
    coef = (solved - pltpu.roll(solved, 64, 1) * share)[:, :members]
    coef = coef - jnp.mean(coef, axis=0, keepdims=True)
    names = lax.broadcasted_iota(jnp.int32, (everyone, members), 0)
    mixing = jnp.zeros((everyone, members), F32)
    for i in range(order):
        mixing = jnp.where(names == near_turned[i : i + 1, :members], coef[i : i + 1], mixing)

    cells = updated.shape[1]
    sources = jnp.concatenate(
        [
            jnp.concatenate([full[slots + HALO : slots + 2 * HALO, members:] for full in fulls], axis=1),
            jnp.concatenate([own[...] for own in owns], axis=1),
            jnp.concatenate([full[slots + EDGE : slots + EDGE + HALO, :members] for full in fulls], axis=1),
        ],
        axis=0,
    )
    field = sources[:, :members] + jnp.dot(
        sources, mixing, precision=lax.Precision.HIGHEST, preferred_element_type=F32
    )
    updated[...] = field[HALO : HALO + cells].T
    run = cells // PARTS
    left, right = end_masks(PARTS, members)
    layers(in_runs(field), run, left, right, taps1, taps2, columns, first, second, heads)
    for q in range(PARTS):
        turned[q * run : (q + 1) * run, :] = heads[:, q * members : (q + 1) * members]
    new_heads[...] = turned[...].T


def from_groups(value):
    groups = lax.axis_size("members")
    found = [value]
    for step in range(1, groups):
        pairs = [((i + step) % groups, i) for i in range(groups)]
        found.append(lax.ppermute(value, "members", pairs))
    return found


def on_device(
    log_field, obs_heads, obs_var, obs_noise, obs_index, obs_count, neighbours,
    lift_gain, lift_bias, conv_first, bias_first, conv_second, bias_second, readout,
):
    members, cells = log_field.shape
    spaces = lax.axis_size("space")
    groups = lax.axis_size("members")
    channels = lift_gain.shape[0]
    slots = obs_var.shape[0]
    order = neighbours.shape[1]

    def work(run, parts):
        rows, lanes = run + 2 * HALO, parts * members
        return (
            pltpu.VMEM((rows, channels, lanes), BF16),
            pltpu.VMEM((rows - 2, channels, lanes), BF16),
            pltpu.VMEM((max(run, 8), lanes), F32),
        )

    own = call(turn_kernel, shape((cells, members)), (log_field,), flops=1 << 34)
    taps1, taps2, columns, near, near_turned, sent = call(
        prepare_kernel,
        (
            shape((channels, 3 * channels), BF16),
            shape((channels + 16, 6 * channels), BF16),
            shape((5, channels, 128)),
            shape((2 * members, 2 * order), jnp.int32),
            shape((2 * order, members), jnp.int32),
            shape((spaces, slots + EDGE, 2 * members)),
        ),
        (
            own, lift_gain, lift_bias, conv_first, bias_first, conv_second, bias_second,
            readout, neighbours, obs_heads, obs_var, obs_noise.T, obs_index, obs_count,
        ),
        scratch=(
            pltpu.VMEM((channels, 3 * channels), F32),
            pltpu.VMEM((channels + 16, 6 * channels), F32),
        )
        + work(cells // PARTS, PARTS),
    )
    got = lax.all_to_all(sent, "space", 0, 0)
    full = call(
        ends_kernel,
        shape((spaces * slots + 2 * EDGE, 2 * members)),
        (got, taps1, taps2, columns),
        scratch=work(2 * HALO, PARTS)
        + (
            pltpu.VMEM((spaces * EDGE, members), F32),
            pltpu.VMEM((8, spaces * slots), F32),
        ),
    )
    return call(
        functools.partial(update_kernel, groups),
        (shape((members, cells)), shape((members, cells))),
        (*from_groups(full), *from_groups(own), taps1, taps2, columns, near, near_turned),
        scratch=(pltpu.VMEM(((order // 2 + 1) * order, 128), F32),)
        + work(cells // PARTS, PARTS)
        + (pltpu.VMEM((cells, members), F32),),
    )


def solution(mesh):
    in_specs = (
        P("members", "space"),
        P("space"),
        P("space"),
        P("members", "space"),
        P("space", None),
        P("space"),
        P("members", None),
        P(),
        P(),
        P(),
        P(),
        P(),
        P(),
        P(),
    )
    out_specs = (P("members", "space"), P("members", "space"))
    return jax.shard_map(
        on_device, mesh=mesh, in_specs=in_specs, out_specs=out_specs, check_vma=False
    )
```

```python
import functools

import jax
import jax.numpy as jnp
from jax import lax
from jax.experimental import pallas as pl
from jax.experimental.pallas import tpu as pltpu
from jax.sharding import PartitionSpec as P

F32 = jnp.float32
BF16 = jnp.bfloat16
HALO = 3
EDGE = 8
PARTS = 4
VMEM = pl.BlockSpec(memory_space=pltpu.VMEM)


def shape(dims, dtype=F32):
    return jax.ShapeDtypeStruct(dims, dtype)


def call(kernel, outs, args, scratch=(), flops=0, limit=40):
    return pl.pallas_call(
        kernel,
        out_shape=outs,
        in_specs=[VMEM] * len(args),
        out_specs=jax.tree.map(lambda _: VMEM, outs),
        scratch_shapes=list(scratch),
        cost_estimate=pl.CostEstimate(flops=flops, bytes_accessed=1 << 18, transcendentals=0),
        compiler_params=pltpu.CompilerParams(vmem_limit_bytes=limit << 20),
    )(*args)


def column(row):
    size = row.shape[1]
    same = lax.broadcasted_iota(jnp.int32, (size, size), 0) == lax.broadcasted_iota(
        jnp.int32, (size, size), 1
    )
    return jnp.sum(jnp.where(same, row, 0.0), axis=1, keepdims=True)


def layers(wide, run, left, right, taps1, taps2, columns, first, second, heads):
    lanes = wide.shape[1]
    rows = run + 2 * HALO
    gain, bias, bias1, bias2, last = [
        jnp.concatenate([columns[i]] * (lanes // columns.shape[2]), axis=1) for i in range(5)
    ]
    channels = gain.shape[0]
    for r in range(rows):
        value = jnp.tanh(gain * wide[r : r + 1] + bias)
        if left is not None and r < HALO:
            value = value * left
        if right is not None and r >= rows - HALO:
            value = value * right
        first[r] = value.astype(BF16)
    for i in range(rows - 2):
        window = first[i : i + 3].reshape(3 * channels, lanes)
        half = jnp.dot(taps1[...], window, preferred_element_type=F32) + bias1
        value = half + half * jnp.tanh(half)
        if left is not None and i < HALO - 1:
            value = value * left
        if right is not None and i >= rows - 2 - (HALO - 1):
            value = value * right
        second[i] = value.astype(BF16)
    split = 3 * channels
    for n in range(run):
        window1 = jnp.concatenate([first[n + 1], first[n + 3], first[n + 5]], axis=0)
        window2 = jnp.concatenate([second[n], second[n + 2], second[n + 4]], axis=0)
        total = jnp.dot(taps2[:, :split], window1, preferred_element_type=F32) + jnp.dot(
            taps2[:, split:], window2, preferred_element_type=F32
        )
        half = total[:channels] + bias2
        third = (half + half * jnp.tanh(half)).astype(BF16).astype(F32)
        rest = jnp.sum(third * last, axis=0, keepdims=True)
        heads[n : n + 1, :] = total[channels : channels + 1] + rest


def in_runs(ext):
    run = (ext.shape[0] - 2 * HALO) // PARTS
    return jnp.concatenate([ext[q * run : (q + 1) * run + 2 * HALO] for q in range(PARTS)], axis=1)


def split3(value):
    one = value.astype(BF16)
    rest = value - one.astype(F32)
    two = rest.astype(BF16)
    three = (rest - two.astype(F32)).astype(BF16)
    return jnp.concatenate([one, two, three], axis=1)


def turn_kernel(field, own):
    own[...] = field[...].T


def end_masks(parts, members):
    space = lax.axis_index("space")
    lane = lax.broadcasted_iota(jnp.int32, (1, parts * members), 1)
    left = (lane < members) & (space == 0)
    right = (lane >= (parts - 1) * members) & (space == lax.axis_size("space") - 1)
    return jnp.where(left, 0.0, 1.0), jnp.where(right, 0.0, 1.0)


def prepare_kernel(
    own, gain, bias, conv1, bias1, conv2, bias2, readout,
    obs_heads, obs_var, noise_turned, obs_index, obs_count,
    taps1, taps2, columns, sent,
    wide1, wide2, first, second, heads,
):
    space = lax.axis_index("space")
    spaces = lax.axis_size("space")
    turned = own[...]
    cells, members = turned.shape
    channels = gain.shape[0]
    split = 3 * channels
    row = readout[...].astype(F32).reshape(1, split)
    wide2[...] = jnp.zeros_like(wide2)
    for tap in range(3):
        at = slice(tap * channels, (tap + 1) * channels)
        wide1[:, at] = 0.5 * conv1[tap].astype(F32)
        both = 0.5 * conv2[tap].astype(F32)
        wide2[0:channels, at] = both[:, :channels]
        wide2[0:channels, split + tap * channels : split + (tap + 1) * channels] = both[:, channels:]
    wide2[channels : channels + 1, channels : 2 * channels] = row[:, :channels]
    wide2[channels : channels + 1, split + channels : split + 2 * channels] = row[
        :, channels : 2 * channels
    ]
    taps1[...] = wide1[...].astype(BF16)
    taps2[...] = wide2[...].astype(BF16)
    rows = [
        gain[...].reshape(1, channels),
        bias[...].reshape(1, channels),
        0.5 * bias1[...].reshape(1, channels),
        0.5 * bias2[...].reshape(1, channels),
        row[:, 2 * channels :],
    ]
    for spot, value in enumerate(rows):
        columns[spot] = jnp.broadcast_to(column(value), (channels, columns.shape[2]))
    slots = obs_var.shape[0]
    cell = obs_index[...]
    low_end = (cell < HALO) & (space > 0)
    high_end = (cell >= cells - HALO) & (space < spaces - 1)
    end_row = jnp.where(
        low_end,
        (space - 1) * EDGE + HALO + cell,
        jnp.where(high_end, space * EDGE + cell - (cells - HALO), -1),
    )
    inside = column(jnp.where(end_row < 0, cell, -1).astype(F32)).astype(jnp.int32)
    chosen = jnp.where(
        lax.broadcasted_iota(jnp.int32, (slots, cells), 1) == inside, 1.0, 0.0
    ).astype(BF16)
    variance = obs_var[...].reshape(1, slots)
    live = lax.broadcasted_iota(jnp.int32, (1, slots), 1) < obs_count[...].reshape(1, 1)
    root_row = jnp.where(live, lax.rsqrt(variance), 0.0)
    root = column(root_row)
    target = column(obs_heads[...].reshape(1, slots))
    wanted = root * (target + jnp.sqrt(column(variance)) * noise_turned[...])

    zeros = jnp.zeros((HALO, members), F32)
    wide = in_runs(jnp.concatenate([zeros, turned, zeros], axis=0))
    left, right = end_masks(PARTS, members)
    layers(wide, cells // PARTS, left, right, taps1, taps2, columns, first, second, heads)
    every = jnp.concatenate(
        [heads[:, q * members : (q + 1) * members] for q in range(PARTS)], axis=0
    )
    parts = jnp.dot(chosen, split3(every), preferred_element_type=F32)
    seen = parts[:, :members] + parts[:, members : 2 * members] + parts[:, 2 * members :]
    weighted = root * seen
    shown = jnp.where(column(jnp.where(end_row < 0, 0.0, 1.0)) > 0.0, root, weighted)
    blank = jnp.zeros((1, 2 * members - slots), F32)
    payload = jnp.concatenate(
        [
            jnp.concatenate([shown, wanted - weighted], axis=1),
            jnp.concatenate([turned[: 2 * HALO], turned[cells - 2 * HALO :]], axis=1),
            jnp.concatenate([end_row.astype(F32), blank], axis=1),
            jnp.zeros((1, 2 * members), F32),
        ],
        axis=0,
    )
    for copy in range(sent.shape[0]):
        sent[copy] = payload


def tables_kernel(neighbours, near, near_turned, choice):
    members, order = neighbours.shape
    everyone = choice.shape[2]
    ids = neighbours[...] - members * lax.axis_index("members")
    ids = jnp.where(ids < 0, ids + everyone, ids)
    pair = jnp.concatenate([ids, ids], axis=1)
    table = jnp.concatenate([pair, pair], axis=0)
    near[...] = table
    turned = pair.T[:order]
    near_turned[...] = jnp.concatenate([turned, turned], axis=1)
    second_half = (lax.broadcasted_iota(jnp.int32, (128, 128), 0) >= 64).astype(jnp.int32)
    everyone_id = lax.broadcasted_iota(jnp.int32, (128, everyone), 1)
    for two in range(order // 2):
        member = jnp.take_along_axis(
            table, 2 * two + second_half, axis=1, mode="promise_in_bounds"
        )
        member = jnp.concatenate([member] * (everyone // 128), axis=1)
        choice[two] = jnp.where(member == everyone_id, 1.0, 0.0).astype(BF16)


def ends_kernel(got, own, taps1, taps2, columns, full, first, second, heads, ends, marks):
    space = lax.axis_index("space")
    spaces = got.shape[0]
    slots = got.shape[1] - EDGE
    members = got.shape[2] // 2
    inner = 2 * HALO
    for start in range(0, spaces, PARTS):
        sides = []
        for here in range(start, start + PARTS):
            there = (here + 1) % spaces
            near_end = got[here, slots : slots + inner, members:]
            far_end = got[there, slots : slots + inner, :members]
            sides.append(jnp.concatenate([near_end, far_end], axis=0))
        wide = jnp.concatenate(sides, axis=1)
        turn = start // PARTS
        layers(
            wide, inner, None, None, taps1, taps2, columns,
            first.at[turn], second.at[turn], heads.at[turn],
        )
        for q in range(PARTS):
            at = (start + q) * EDGE
            ends[at : at + EDGE, :] = heads[turn, :, q * members : (q + 1) * members]
    for tile in range(spaces):
        at = tile * slots
        marks[0:1, at : at + slots] = got[tile, slots + inner : slots + inner + 1, :slots]
    row = lax.broadcasted_iota(jnp.int32, (spaces * EDGE, spaces * slots), 0).astype(F32)
    picks = jnp.where(row == marks[0:1, :], 1.0, 0.0).astype(BF16)
    exact = split3(ends[...])
    exact = [exact[:, i * members : (i + 1) * members] for i in range(3)]
    flag = jnp.ones((spaces * EDGE, 2 * members), BF16)
    none = jnp.zeros((spaces * EDGE, 2 * members), BF16)
    table = jnp.concatenate(
        [
            jnp.concatenate([part, part, flag if i == 0 else none], axis=1)
            for i, part in enumerate(exact)
        ],
        axis=0,
    )
    parts = lax.dot_general(
        jnp.concatenate([picks] * 3, axis=0), table, (((0,), (0,)), ((), ())),
        preferred_element_type=F32,
    )
    heads_lane = lax.broadcasted_iota(jnp.int32, (1, 2 * members), 1) < members
    for tile in range(spaces):
        at = slice(tile * slots, (tile + 1) * slots)
        there = got[tile, :slots, :]
        shown = jnp.where(heads_lane, there, pltpu.roll(there, members, 1))
        seen, marked = parts[at, : 2 * members], parts[at, 2 * members :]
        full[at, :] = jnp.where(
            heads_lane, shown * (1.0 - marked + seen), there - shown * seen
        )
    before = jnp.where(space == 0, spaces - 1, space - 1)
    after = jnp.where(space == spaces - 1, 0, space + 1)
    at = spaces * slots
    full[at : at + EDGE, :] = got[before, slots:, :]
    full[at + EDGE : at + 2 * EDGE, :] = got[after, slots:, :]
    half = own.shape[0] // 2
    full[at + 2 * EDGE :, :] = jnp.concatenate([own[:half, :], own[half:, :]], axis=1)


def lane_gather(table, index):
    low = index & 127
    high = index >> 7
    found = None
    for tile in range(table.shape[1] // 128):
        part = jnp.take_along_axis(
            table[:, tile * 128 : (tile + 1) * 128], low, axis=1, mode="promise_in_bounds"
        )
        found = part if found is None else jnp.where(high == tile, part, found)
    return found


def update_kernel(groups, *refs):
    fulls = refs[:groups]
    (
        taps1, taps2, columns, near, near_turned, choice,
        updated, new_heads,
        system, first, second, heads, turned,
    ) = refs[groups:]
    cells = updated.shape[1]
    slots = fulls[0].shape[0] - 2 * EDGE - cells // 2
    members = fulls[0].shape[1] // 2
    everyone = groups * members
    order = near.shape[0] // 2
    half_lane = lax.broadcasted_iota(jnp.int32, (1, 128), 1) < 64

    panel = jnp.concatenate([full[0:slots, :members] for full in fulls], axis=1)
    panel = panel - jnp.mean(panel, axis=1, keepdims=True)
    innovation = fulls[0][0:slots, members:]
    stacked = jnp.concatenate([panel, innovation], axis=1)
    product = lax.dot_general(
        stacked, panel, (((0,), (0,)), ((), ())),
        precision=lax.Precision.HIGHEST, preferred_element_type=F32,
    )
    gram = split3(product[:everyone])
    sides = product[everyone:]

    ids = near[...]
    lane_id = lax.broadcasted_iota(jnp.int32, (128, 128), 1)
    row_id = lax.broadcasted_iota(jnp.int32, (128, 128), 0)

    def extract(quad, carry):
        found = []
        for b in range(2):
            parts = jnp.dot(choice[2 * quad + b], gram, preferred_element_type=F32)
            rows = (
                parts[:, :everyone]
                + parts[:, everyone : 2 * everyone]
                + parts[:, 2 * everyone :]
            )
            found.append(lane_gather(rows, ids))
        block = jnp.where(half_lane, found[0], found[1]).T
        own = 4 * quad + 2 * (row_id >= 64).astype(jnp.int32) + (lane_id >= 64).astype(jnp.int32)
        block = block + jnp.where((row_id & 63) == own, order - 1.0, 0.0)
        system[pl.ds(pl.multiple_of(quad * 128, 128), 128), :] = block
        return carry

    lax.fori_loop(0, order // 4, extract, 0, unroll=order // 4)
    side = lane_gather(jnp.concatenate([sides, sides], axis=0), ids)
    side = jnp.where(row_id >= 64, 1.0, side).T[:order]
    system[order // 2 * order : (order // 2 + 1) * order, :] = side

    blocks = order // 2
    def both(value):
        turn = pltpu.roll(value, 64, 1)
        return jnp.where(half_lane, value, turn), jnp.where(half_lane, turn, value)

    def without(value, pair):
        at = 2 * pair // 8 * 8
        row = lax.broadcasted_iota(jnp.int32, (8, 128), 0) + at
        tile = jnp.where((row >= 2 * pair) & (row < 2 * pair + 2), 0.0, value[at : at + 8])
        parts = [value[:at], tile, value[at + 8 :]]
        return jnp.concatenate([part for part in parts if part.shape[0]], axis=0)

    def factors(col0, col1, pair):
        one, two = 2 * pair, 2 * pair + 1
        d, e, f = col0[one:two], col1[one:two], col1[two : two + 1]
        inv = 1.0 / (d * f - e * e)
        fac0 = without((col0 * f - col1 * e) * inv, pair)
        fac1 = without((col1 * d - col0 * e) * inv, pair)
        return fac0, fac1, (f * inv, d * inv, e * inv)

    own_share, cross_share = [], []
    fac0, fac1, shares = factors(*both(system[0:order, :]), 0)
    for pair in range(blocks):
        own_share += [shares[0], shares[1]]
        cross_share += [shares[2], shares[2]]
        one, two = 2 * pair, 2 * pair + 1
        if pair + 1 < blocks:
            col0, col1 = both(system[(pair + 1) * order : (pair + 2) * order, :])
            later = factors(
                col0 - fac0 * col0[one:two] - fac1 * col0[two : two + 1],
                col1 - fac0 * col1[one:two] - fac1 * col1[two : two + 1],
                pair + 1,
            )
        for block in range(min(pair + 2, blocks), blocks + 1):
            at = block * order
            row0 = system[at + one : at + two, :]
            row1 = system[at + two : at + two + 1, :]
            system[at : at + order, :] = system[at : at + order, :] - fac0 * row0 - fac1 * row1
        if pair + 1 < blocks:
            fac0, fac1, shares = later
    sides = system[blocks * order :, :]
    even = lax.broadcasted_iota(jnp.int32, (order, 128), 0) % 2 == 0
    partner = jnp.where(even, pltpu.roll(sides, order - 1, 0), pltpu.roll(sides, 1, 0))
    solved = sides * jnp.concatenate(own_share, axis=0) - partner * jnp.concatenate(
        cross_share, axis=0
    )
    sums = jnp.sum(solved, axis=0, keepdims=True)
    share = sums / pltpu.roll(sums, 64, 1)
    coef = (solved - pltpu.roll(solved, 64, 1) * share)[:, :members]
    coef = coef - jnp.mean(coef, axis=0, keepdims=True)
    coef = jnp.concatenate([coef, coef], axis=1)
    name = lax.broadcasted_iota(jnp.int32, (everyone // 2, 128), 0) + jnp.where(
        half_lane, 0, everyone // 2
    )
    mixing = jnp.zeros((everyone // 2, 128), F32)
    for i in range(order):
        mixing = jnp.where(name == near_turned[i : i + 1, :], coef[i : i + 1], mixing)
    mixing = jnp.concatenate([mixing[:, :members], mixing[:, members:]], axis=0)

    before, after, body = slots, slots + EDGE, slots + 2 * EDGE
    sources = jnp.concatenate(
        [
            jnp.concatenate([full[before + HALO : before + 2 * HALO, members:] for full in fulls], axis=1),
            jnp.concatenate([full[body:, :members] for full in fulls], axis=1),
            jnp.concatenate([full[body:, members:] for full in fulls], axis=1),
            jnp.concatenate([full[after : after + HALO, :members] for full in fulls], axis=1),
        ],
        axis=0,
    )
    field = sources[:, :members] + jnp.dot(
        sources, mixing, precision=lax.Precision.HIGHEST, preferred_element_type=F32
    )
    updated[...] = field[HALO : HALO + cells].T
    run = cells // PARTS
    left, right = end_masks(PARTS, members)
    layers(in_runs(field), run, left, right, taps1, taps2, columns, first, second, heads)
    for q in range(PARTS):
        turned[q * run : (q + 1) * run, :] = heads[:, q * members : (q + 1) * members]
    new_heads[...] = turned[...].T


def from_groups(value):
    groups = lax.axis_size("members")
    found = [value]
    for step in range(1, groups):
        pairs = [((i + step) % groups, i) for i in range(groups)]
        found.append(lax.ppermute(value, "members", pairs))
    return found


def on_device(
    log_field, obs_heads, obs_var, obs_noise, obs_index, obs_count, neighbours,
    lift_gain, lift_bias, conv_first, bias_first, conv_second, bias_second, readout,
):
    members, cells = log_field.shape
    spaces = lax.axis_size("space")
    groups = lax.axis_size("members")
    channels = lift_gain.shape[0]
    slots = obs_var.shape[0]
    order = neighbours.shape[1]

    def work(run, parts):
        rows, lanes = run + 2 * HALO, parts * members
        return (
            pltpu.VMEM((rows, channels, lanes), BF16),
            pltpu.VMEM((rows - 2, channels, lanes), BF16),
            pltpu.VMEM((max(run, 8), lanes), F32),
        )

    own = call(turn_kernel, shape((cells, members)), (log_field,), flops=1 << 34)
    taps1, taps2, columns, sent = call(
        prepare_kernel,
        (
            shape((channels, 3 * channels), BF16),
            shape((channels + 16, 6 * channels), BF16),
            shape((5, channels, 128)),
            shape((spaces, slots + EDGE, 2 * members)),
        ),
        (
            own, lift_gain, lift_bias, conv_first, bias_first, conv_second, bias_second,
            readout, obs_heads, obs_var, obs_noise.T, obs_index, obs_count,
        ),
        scratch=(
            pltpu.VMEM((channels, 3 * channels), F32),
            pltpu.VMEM((channels + 16, 6 * channels), F32),
        )
        + work(cells // PARTS, PARTS),
    )
    got = lax.all_to_all(sent, "space", 0, 0)
    near, near_turned, choice = call(
        tables_kernel,
        (
            shape((2 * members, 2 * order), jnp.int32),
            shape((order, 2 * members), jnp.int32),
            shape((order // 2, 2 * members, groups * members), BF16),
        ),
        (neighbours,),
        flops=1 << 30,
    )
    turns = spaces // PARTS
    full = call(
        ends_kernel,
        shape((spaces * slots + 2 * EDGE + cells // 2, 2 * members)),
        (got, own, taps1, taps2, columns),
        scratch=tuple(
            pltpu.VMEM((turns, *value.shape), value.dtype) for value in work(2 * HALO, PARTS)
        )
        + (
            pltpu.VMEM((spaces * EDGE, members), F32),
            pltpu.VMEM((8, spaces * slots), F32),
        ),
    )
    return call(
        functools.partial(update_kernel, groups),
        (shape((members, cells)), shape((members, cells))),
        (*from_groups(full), taps1, taps2, columns, near, near_turned, choice),
        scratch=(pltpu.VMEM(((order // 2 + 1) * order, 128), F32),)
        + work(cells // PARTS, PARTS)
        + (pltpu.VMEM((cells, members), F32),),
    )


def solution(mesh):
    in_specs = (
        P("members", "space"),
        P("space"),
        P("space"),
        P("members", "space"),
        P("space", None),
        P("space"),
        P("members", None),
        P(),
        P(),
        P(),
        P(),
        P(),
        P(),
        P(),
    )
    out_specs = (P("members", "space"), P("members", "space"))
    return jax.shard_map(
        on_device, mesh=mesh, in_specs=in_specs, out_specs=out_specs, check_vma=False
    )
```

```python
import functools

import jax
import jax.numpy as jnp
from jax import lax
from jax.experimental import pallas as pl
from jax.experimental.pallas import tpu as pltpu
from jax.sharding import PartitionSpec as P

F32 = jnp.float32
BF16 = jnp.bfloat16
HALO = 3
EDGE = 8
PARTS = 4
BAND = 3
VMEM = pl.BlockSpec(memory_space=pltpu.VMEM)


def shape(dims, dtype=F32):
    return jax.ShapeDtypeStruct(dims, dtype)


def call(kernel, outs, args, scratch=(), flops=0, limit=40):
    return pl.pallas_call(
        kernel,
        out_shape=outs,
        in_specs=[VMEM] * len(args),
        out_specs=jax.tree.map(lambda _: VMEM, outs),
        scratch_shapes=list(scratch),
        cost_estimate=pl.CostEstimate(flops=flops, bytes_accessed=1 << 18, transcendentals=0),
        compiler_params=pltpu.CompilerParams(vmem_limit_bytes=limit << 20),
    )(*args)


def column(row):
    size = row.shape[1]
    same = lax.broadcasted_iota(jnp.int32, (size, size), 0) == lax.broadcasted_iota(
        jnp.int32, (size, size), 1
    )
    return jnp.sum(jnp.where(same, row, 0.0), axis=1, keepdims=True)


def groups_of(count):
    return [min(at, count - BAND) for at in range(0, count, BAND)]


def layers(wide, run, left, right, taps1, taps2, columns, first, second, heads):
    lanes = wide.shape[1]
    rows = run + 2 * HALO
    gain, bias, bias1, bias2, last = [
        jnp.concatenate([columns[i]] * (lanes // columns.shape[2]), axis=1) for i in range(5)
    ]
    channels = gain.shape[0]
    for r in range(rows):
        value = jnp.tanh(gain * wide[r : r + 1] + bias)
        if left is not None and r < HALO:
            value = value * left
        if right is not None and r >= rows - HALO:
            value = value * right
        first[r] = value.astype(BF16)
    reach = BAND + 2
    for start in groups_of(rows - 2):
        window = first[start : start + reach].reshape(reach * channels, lanes)
        total = jnp.dot(taps1[...], window, preferred_element_type=F32)
        for r in range(BAND):
            i = start + r
            half = total[r * channels : (r + 1) * channels] + bias1
            value = half + half * jnp.tanh(half)
            if left is not None and i < HALO - 1:
                value = value * left
            if right is not None and i >= rows - 2 - (HALO - 1):
                value = value * right
            second[i] = value.astype(BF16)
    split = reach * channels
    for parity in range(2):
        for group in groups_of(run // 2):
            start = 2 * group + parity
            near = [first[start + 1 + 2 * i] for i in range(reach)]
            far = [second[start + 2 * i] for i in range(reach)]
            total = jnp.dot(
                taps2[:, :split], jnp.concatenate(near, axis=0), preferred_element_type=F32
            ) + jnp.dot(taps2[:, split:], jnp.concatenate(far, axis=0), preferred_element_type=F32)
            for r in range(BAND):
                n = start + 2 * r
                half = total[r * channels : (r + 1) * channels] + bias2
                third = (half + half * jnp.tanh(half)).astype(BF16).astype(F32)
                rest = jnp.sum(third * last, axis=0, keepdims=True)
                at = BAND * channels + r
                heads[n : n + 1, :] = total[at : at + 1] + rest


def in_runs(ext):
    run = (ext.shape[0] - 2 * HALO) // PARTS
    return jnp.concatenate([ext[q * run : (q + 1) * run + 2 * HALO] for q in range(PARTS)], axis=1)


def split3(value):
    one = value.astype(BF16)
    rest = value - one.astype(F32)
    two = rest.astype(BF16)
    three = (rest - two.astype(F32)).astype(BF16)
    return jnp.concatenate([one, two, three], axis=1)


def blank_kernel(blank):
    blank[...] = jnp.zeros_like(blank)


def end_masks(parts, members):
    space = lax.axis_index("space")
    lane = lax.broadcasted_iota(jnp.int32, (1, parts * members), 1)
    left = (lane < members) & (space == 0)
    right = (lane >= (parts - 1) * members) & (space == lax.axis_size("space") - 1)
    return jnp.where(left, 0.0, 1.0), jnp.where(right, 0.0, 1.0)


def prepare_kernel(
    empty, field, gain, bias, conv1, bias1, conv2, bias2, readout,
    obs_heads, obs_var, noise_turned, obs_index, obs_count,
    own, taps1, taps2, columns, sent,
    wide1, wide2, first, second, heads,
):
    space = lax.axis_index("space")
    spaces = lax.axis_size("space")
    turned = field[...].T
    own[...] = turned
    cells, members = turned.shape
    channels = gain.shape[0]
    row = readout[...].astype(F32).reshape(1, 3 * channels)
    split = (BAND + 2) * channels
    wide1[...] = jnp.zeros_like(wide1)
    wide2[...] = jnp.zeros_like(wide2)
    for tap in range(3):
        one = 0.5 * conv1[tap].astype(F32)
        both = 0.5 * conv2[tap].astype(F32)
        for r in range(BAND):
            out = slice(r * channels, (r + 1) * channels)
            at = (r + tap) * channels
            wide1[out, at : at + channels] = one
            wide2[out, at : at + channels] = both[:, :channels]
            wide2[out, split + at : split + at + channels] = both[:, channels:]
    for r in range(BAND):
        out, at = BAND * channels + r, (r + 1) * channels
        wide2[out : out + 1, at : at + channels] = row[:, :channels]
        wide2[out : out + 1, split + at : split + at + channels] = row[:, channels : 2 * channels]
    taps1[...] = wide1[...].astype(BF16)
    taps2[...] = wide2[...].astype(BF16)
    rows = [
        gain[...].reshape(1, channels),
        bias[...].reshape(1, channels),
        0.5 * bias1[...].reshape(1, channels),
        0.5 * bias2[...].reshape(1, channels),
        row[:, 2 * channels :],
    ]
    for spot, value in enumerate(rows):
        columns[spot] = jnp.broadcast_to(column(value), (channels, columns.shape[2]))
    slots = obs_var.shape[0]
    cell = obs_index[...]
    low_end = (cell < HALO) & (space > 0)
    high_end = (cell >= cells - HALO) & (space < spaces - 1)
    end_row = jnp.where(
        low_end,
        (space - 1) * EDGE + HALO + cell,
        jnp.where(high_end, space * EDGE + cell - (cells - HALO), -1),
    )
    inside = column(jnp.where(end_row < 0, cell, -1).astype(F32)).astype(jnp.int32)
    chosen = jnp.where(
        lax.broadcasted_iota(jnp.int32, (slots, cells), 1) == inside, 1.0, 0.0
    ).astype(BF16)
    variance = obs_var[...].reshape(1, slots)
    live = lax.broadcasted_iota(jnp.int32, (1, slots), 1) < obs_count[...].reshape(1, 1)
    root_row = jnp.where(live, lax.rsqrt(variance), 0.0)
    root = column(root_row)
    target = column(obs_heads[...].reshape(1, slots))
    wanted = root * (target + jnp.sqrt(column(variance)) * noise_turned[...])

    zeros = jnp.zeros((HALO, members), F32)
    wide = in_runs(jnp.concatenate([zeros, turned, zeros], axis=0))
    left, right = end_masks(PARTS, members)
    layers(wide, cells // PARTS, left, right, taps1, taps2, columns, first, second, heads)
    every = jnp.concatenate(
        [heads[:, q * members : (q + 1) * members] for q in range(PARTS)], axis=0
    )
    parts = jnp.dot(chosen, split3(every), preferred_element_type=F32)
    seen = parts[:, :members] + parts[:, members : 2 * members] + parts[:, 2 * members :]
    weighted = root * seen
    shown = jnp.where(column(jnp.where(end_row < 0, 0.0, 1.0)) > 0.0, root, weighted)
    blank = empty[0:1, slots : 2 * members]
    payload = jnp.concatenate(
        [
            jnp.concatenate([shown, wanted - weighted], axis=1),
            jnp.concatenate([turned[: 2 * HALO], turned[cells - 2 * HALO :]], axis=1),
            jnp.concatenate([end_row.astype(F32), blank], axis=1),
            jnp.zeros((1, 2 * members), F32),
        ],
        axis=0,
    )
    for copy in range(sent.shape[0]):
        sent[copy] = payload


def tables_kernel(neighbours, near, near_turned, choice):
    members, order = neighbours.shape
    everyone = choice.shape[2]
    ids = neighbours[...] - members * lax.axis_index("members")
    ids = jnp.where(ids < 0, ids + everyone, ids)
    pair = jnp.concatenate([ids, ids], axis=1)
    table = jnp.concatenate([pair, pair], axis=0)
    near[...] = table
    turned = pair.T[:order]
    near_turned[...] = jnp.concatenate([turned, turned], axis=1)
    second_half = (lax.broadcasted_iota(jnp.int32, (128, 128), 0) >= 64).astype(jnp.int32)
    everyone_id = lax.broadcasted_iota(jnp.int32, (128, everyone), 1)
    for two in range(order // 2):
        member = jnp.take_along_axis(
            table, 2 * two + second_half, axis=1, mode="promise_in_bounds"
        )
        member = jnp.concatenate([member] * (everyone // 128), axis=1)
        choice[two] = jnp.where(member == everyone_id, 1.0, 0.0).astype(BF16)


def ends_kernel(
    got, own, taps1, taps2, columns,
    kept, swapped, first, second, heads, ends, marks,
):
    space = lax.axis_index("space")
    spaces = got.shape[0]
    slots = got.shape[1] - EDGE
    members = got.shape[2] // 2
    inner = 2 * HALO
    for start in range(0, spaces, PARTS):
        sides = []
        for here in range(start, start + PARTS):
            there = (here + 1) % spaces
            near_end = got[here, slots : slots + inner, members:]
            far_end = got[there, slots : slots + inner, :members]
            sides.append(jnp.concatenate([near_end, far_end], axis=0))
        wide = jnp.concatenate(sides, axis=1)
        turn = start // PARTS
        layers(
            wide, inner, None, None, taps1, taps2, columns,
            first.at[turn], second.at[turn], heads.at[turn],
        )
        for q in range(PARTS):
            at = (start + q) * EDGE
            ends[at : at + EDGE, :] = heads[turn, :, q * members : (q + 1) * members]
    for tile in range(spaces):
        at = tile * slots
        marks[0:1, at : at + slots] = got[tile, slots + inner : slots + inner + 1, :slots]
    row = lax.broadcasted_iota(jnp.int32, (spaces * EDGE, spaces * slots), 0).astype(F32)
    picks = jnp.where(row == marks[0:1, :], 1.0, 0.0).astype(BF16)
    exact = split3(ends[...])
    exact = [exact[:, i * members : (i + 1) * members] for i in range(3)]
    flag = jnp.ones((spaces * EDGE, 2 * members), BF16)
    none = jnp.zeros((spaces * EDGE, 2 * members), BF16)
    table = jnp.concatenate(
        [
            jnp.concatenate([part, part, flag if i == 0 else none], axis=1)
            for i, part in enumerate(exact)
        ],
        axis=0,
    )
    parts = lax.dot_general(
        jnp.concatenate([picks] * 3, axis=0), table, (((0,), (0,)), ((), ())),
        preferred_element_type=F32,
    )
    heads_lane = lax.broadcasted_iota(jnp.int32, (1, 2 * members), 1) < members
    half = spaces * slots // 2

    def finished(tile):
        at = slice(tile * slots, (tile + 1) * slots)
        there = got[tile, :slots, :]
        shown = jnp.where(heads_lane, there, pltpu.roll(there, members, 1))
        seen, marked = parts[at, : 2 * members], parts[at, 2 * members :]
        return jnp.where(heads_lane, shown * (1.0 - marked + seen), there - shown * seen)

    for tile in range(spaces // 2):
        at = slice(tile * slots, (tile + 1) * slots)
        one, two = finished(tile), finished(tile + spaces // 2)
        kept[at, :] = one
        kept[half + tile * slots : half + (tile + 1) * slots, :] = two
        swapped[at, :] = jnp.where(heads_lane, one, pltpu.roll(two, members, 1))
    before = jnp.where(space == 0, spaces - 1, space - 1)
    after = jnp.where(space == spaces - 1, 0, space + 1)
    swapped[half : half + EDGE, :] = got[before, slots:, :]
    swapped[half + EDGE : half + 2 * EDGE, :] = got[after, slots:, :]
    middle = own.shape[0] // 2
    swapped[half + 2 * EDGE :, :] = jnp.concatenate([own[:middle, :], own[middle:, :]], axis=1)


def lane_gather(table, index):
    low = index & 127
    high = index >> 7
    found = None
    for tile in range(table.shape[1] // 128):
        part = jnp.take_along_axis(
            table[:, tile * 128 : (tile + 1) * 128], low, axis=1, mode="promise_in_bounds"
        )
        found = part if found is None else jnp.where(high == tile, part, found)
    return found


def update_kernel(groups, *refs):
    kept, parcels = refs[0], refs[1 : 1 + groups]
    (
        taps1, taps2, columns, near, near_turned, choice,
        updated, new_heads,
        system, first, second, heads, turned,
    ) = refs[1 + groups :]
    cells = updated.shape[1]
    slots, members = kept.shape[0], kept.shape[1] // 2
    everyone = groups * members
    order = near.shape[0] // 2
    half_lane = lax.broadcasted_iota(jnp.int32, (1, 128), 1) < 64

    panel = []
    for g in range(0, groups, 2):
        right = parcels[g + 1][0 : slots // 2, :]
        right = jnp.concatenate([pltpu.roll(right, members, 1), right], axis=0)
        if g:
            left = parcels[g][0 : slots // 2, :]
            left = jnp.concatenate([left, pltpu.roll(left, members, 1)], axis=0)
        else:
            left = kept[...]
        panel.append(jnp.where(half_lane, left, right))
    panel = jnp.concatenate(panel, axis=1)
    panel = panel - jnp.mean(panel, axis=1, keepdims=True)
    innovation = kept[:, members:]
    stacked = jnp.concatenate([panel, innovation], axis=1)
    product = lax.dot_general(
        stacked, panel, (((0,), (0,)), ((), ())),
        precision=lax.Precision.HIGHEST, preferred_element_type=F32,
    )
    gram = split3(product[:everyone])
    sides = product[everyone:]

    ids = near[...]
    lane_id = lax.broadcasted_iota(jnp.int32, (128, 128), 1)
    row_id = lax.broadcasted_iota(jnp.int32, (128, 128), 0)

    def extract(quad, carry):
        found = []
        for b in range(2):
            parts = jnp.dot(choice[2 * quad + b], gram, preferred_element_type=F32)
            rows = (
                parts[:, :everyone]
                + parts[:, everyone : 2 * everyone]
                + parts[:, 2 * everyone :]
            )
            found.append(lane_gather(rows, ids))
        block = jnp.where(half_lane, found[0], found[1]).T
        own = 4 * quad + 2 * (row_id >= 64).astype(jnp.int32) + (lane_id >= 64).astype(jnp.int32)
        block = block + jnp.where((row_id & 63) == own, order - 1.0, 0.0)
        system[pl.ds(pl.multiple_of(quad * 128, 128), 128), :] = block
        return carry

    lax.fori_loop(0, order // 4, extract, 0, unroll=order // 4)
    side = lane_gather(jnp.concatenate([sides, sides], axis=0), ids)
    side = jnp.where(row_id >= 64, 1.0, side).T[:order]
    system[order // 2 * order : (order // 2 + 1) * order, :] = side

    blocks = order // 2
    def both(value):
        turn = pltpu.roll(value, 64, 1)
        return jnp.where(half_lane, value, turn), jnp.where(half_lane, turn, value)

    def without(value, pair):
        at = 2 * pair // 8 * 8
        row = lax.broadcasted_iota(jnp.int32, (8, 128), 0) + at
        tile = jnp.where((row >= 2 * pair) & (row < 2 * pair + 2), 0.0, value[at : at + 8])
        parts = [value[:at], tile, value[at + 8 :]]
        return jnp.concatenate([part for part in parts if part.shape[0]], axis=0)

    def factors(col0, col1, pair):
        one, two = 2 * pair, 2 * pair + 1
        d, e, f = col0[one:two], col1[one:two], col1[two : two + 1]
        inv = 1.0 / (d * f - e * e)
        fac0 = without((col0 * f - col1 * e) * inv, pair)
        fac1 = without((col1 * d - col0 * e) * inv, pair)
        return fac0, fac1, (f * inv, d * inv, e * inv)

    own_share, cross_share = [], []
    fac0, fac1, shares = factors(*both(system[0:order, :]), 0)
    for pair in range(blocks):
        own_share += [shares[0], shares[1]]
        cross_share += [shares[2], shares[2]]
        one, two = 2 * pair, 2 * pair + 1
        if pair + 1 < blocks:
            col0, col1 = both(system[(pair + 1) * order : (pair + 2) * order, :])
            later = factors(
                col0 - fac0 * col0[one:two] - fac1 * col0[two : two + 1],
                col1 - fac0 * col1[one:two] - fac1 * col1[two : two + 1],
                pair + 1,
            )
        for block in range(min(pair + 2, blocks), blocks + 1):
            at = block * order
            row0 = system[at + one : at + two, :]
            row1 = system[at + two : at + two + 1, :]
            system[at : at + order, :] = system[at : at + order, :] - fac0 * row0 - fac1 * row1
        if pair + 1 < blocks:
            fac0, fac1, shares = later
    sides = system[blocks * order :, :]
    even = lax.broadcasted_iota(jnp.int32, (order, 128), 0) % 2 == 0
    partner = jnp.where(even, pltpu.roll(sides, order - 1, 0), pltpu.roll(sides, 1, 0))
    solved = sides * jnp.concatenate(own_share, axis=0) - partner * jnp.concatenate(
        cross_share, axis=0
    )
    sums = jnp.sum(solved, axis=0, keepdims=True)
    share = sums / pltpu.roll(sums, 64, 1)
    coef = (solved - pltpu.roll(solved, 64, 1) * share)[:, :members]
    coef = coef - jnp.mean(coef, axis=0, keepdims=True)
    coef = jnp.concatenate([coef, coef], axis=1)
    name = lax.broadcasted_iota(jnp.int32, (everyone // 2, 128), 0) + jnp.where(
        half_lane, 0, everyone // 2
    )
    mixing = jnp.zeros((everyone // 2, 128), F32)
    for i in range(order):
        mixing = jnp.where(name == near_turned[i : i + 1, :], coef[i : i + 1], mixing)
    mixing = jnp.concatenate([mixing[:, :members], mixing[:, members:]], axis=0)

    before = slots // 2
    after, body = before + EDGE, before + 2 * EDGE
    sources = jnp.concatenate(
        [
            jnp.concatenate([full[before + HALO : before + 2 * HALO, members:] for full in parcels], axis=1),
            jnp.concatenate([full[body:, :members] for full in parcels], axis=1),
            jnp.concatenate([full[body:, members:] for full in parcels], axis=1),
            jnp.concatenate([full[after : after + HALO, :members] for full in parcels], axis=1),
        ],
        axis=0,
    )
    field = sources[:, :members] + jnp.dot(
        sources, mixing, precision=lax.Precision.HIGHEST, preferred_element_type=F32
    )
    updated[...] = field[HALO : HALO + cells].T
    run = cells // PARTS
    left, right = end_masks(PARTS, members)
    layers(in_runs(field), run, left, right, taps1, taps2, columns, first, second, heads)
    for q in range(PARTS):
        turned[q * run : (q + 1) * run, :] = heads[:, q * members : (q + 1) * members]
    new_heads[...] = turned[...].T


def from_groups(value):
    groups = lax.axis_size("members")
    found = [value]
    for step in range(1, groups):
        pairs = [((i + step) % groups, i) for i in range(groups)]
        found.append(lax.ppermute(value, "members", pairs))
    return found


def on_device(
    log_field, obs_heads, obs_var, obs_noise, obs_index, obs_count, neighbours,
    lift_gain, lift_bias, conv_first, bias_first, conv_second, bias_second, readout,
):
    members, cells = log_field.shape
    spaces = lax.axis_size("space")
    groups = lax.axis_size("members")
    channels = lift_gain.shape[0]
    slots = obs_var.shape[0]
    order = neighbours.shape[1]

    def work(run, parts):
        rows, lanes = run + 2 * HALO, parts * members
        return (
            pltpu.VMEM((rows, channels, lanes), BF16),
            pltpu.VMEM((rows - 2, channels, lanes), BF16),
            pltpu.VMEM((max(run, 8), lanes), F32),
        )

    reach = (BAND + 2) * channels
    empty = call(blank_kernel, shape((8, 2 * members)), (), flops=1 << 34)
    own, taps1, taps2, columns, sent = call(
        prepare_kernel,
        (
            shape((cells, members)),
            shape((BAND * channels, reach), BF16),
            shape((BAND * channels + 16, 2 * reach), BF16),
            shape((5, channels, 128)),
            shape((spaces, slots + EDGE, 2 * members)),
        ),
        (
            empty, log_field, lift_gain, lift_bias, conv_first, bias_first, conv_second, bias_second,
            readout, obs_heads, obs_var, obs_noise.T, obs_index, obs_count,
        ),
        scratch=(
            pltpu.VMEM((BAND * channels, reach), F32),
            pltpu.VMEM((BAND * channels + 16, 2 * reach), F32),
        )
        + work(cells // PARTS, PARTS),
    )
    got = lax.all_to_all(sent, "space", 0, 0)
    near, near_turned, choice = call(
        tables_kernel,
        (
            shape((2 * members, 2 * order), jnp.int32),
            shape((order, 2 * members), jnp.int32),
            shape((order // 2, 2 * members, groups * members), BF16),
        ),
        (neighbours,),
        flops=1 << 30,
    )
    turns = spaces // PARTS
    kept, swapped = call(
        ends_kernel,
        (
            shape((spaces * slots, 2 * members)),
            shape((spaces * slots // 2 + 2 * EDGE + cells // 2, 2 * members)),
        ),
        (got, own, taps1, taps2, columns),
        scratch=tuple(
            pltpu.VMEM((turns, *value.shape), value.dtype) for value in work(2 * HALO, PARTS)
        )
        + (
            pltpu.VMEM((spaces * EDGE, members), F32),
            pltpu.VMEM((8, spaces * slots), F32),
        ),
    )
    return call(
        functools.partial(update_kernel, groups),
        (shape((members, cells)), shape((members, cells))),
        (kept, *from_groups(swapped), taps1, taps2, columns, near, near_turned, choice),
        scratch=(pltpu.VMEM(((order // 2 + 1) * order, 128), F32),)
        + work(cells // PARTS, PARTS)
        + (pltpu.VMEM((cells, members), F32),),
    )


def solution(mesh):
    in_specs = (
        P("members", "space"),
        P("space"),
        P("space"),
        P("members", "space"),
        P("space", None),
        P("space"),
        P("members", None),
        P(),
        P(),
        P(),
        P(),
        P(),
        P(),
        P(),
    )
    out_specs = (P("members", "space"), P("members", "space"))
    return jax.shard_map(
        on_device, mesh=mesh, in_specs=in_specs, out_specs=out_specs, check_vma=False
    )
```

```python
import functools

import jax
import jax.numpy as jnp
from jax import lax
from jax.experimental import pallas as pl
from jax.experimental.pallas import tpu as pltpu
from jax.sharding import PartitionSpec as P

F32 = jnp.float32
BF16 = jnp.bfloat16
HALO = 3
EDGE = 8
PARTS = 4
BAND = 3
VMEM = pl.BlockSpec(memory_space=pltpu.VMEM)


def shape(dims, dtype=F32):
    return jax.ShapeDtypeStruct(dims, dtype)


def call(kernel, outs, args, scratch=(), flops=0, limit=40):
    return pl.pallas_call(
        kernel,
        out_shape=outs,
        in_specs=[VMEM] * len(args),
        out_specs=jax.tree.map(lambda _: VMEM, outs),
        scratch_shapes=list(scratch),
        cost_estimate=pl.CostEstimate(flops=flops, bytes_accessed=1 << 18, transcendentals=0),
        compiler_params=pltpu.CompilerParams(vmem_limit_bytes=limit << 20),
    )(*args)


def column(row):
    size = row.shape[1]
    same = lax.broadcasted_iota(jnp.int32, (size, size), 0) == lax.broadcasted_iota(
        jnp.int32, (size, size), 1
    )
    return jnp.sum(jnp.where(same, row, 0.0), axis=1, keepdims=True)


def groups_of(count):
    return [min(at, count - BAND) for at in range(0, count, BAND)]


def layers(wide, run, left, right, taps1, taps2, columns, first, second, heads):
    lanes = wide.shape[1]
    rows = run + 2 * HALO
    gain, bias, bias1, bias2, last = [
        jnp.concatenate([columns[i]] * (lanes // columns.shape[2]), axis=1) for i in range(5)
    ]
    channels = gain.shape[0]
    for r in range(rows):
        value = jnp.tanh(gain * wide[r : r + 1] + bias)
        if left is not None and r < HALO:
            value = value * left
        if right is not None and r >= rows - HALO:
            value = value * right
        first[r] = value.astype(BF16)
    reach = BAND + 2
    for start in groups_of(rows - 2):
        window = first[start : start + reach].reshape(reach * channels, lanes)
        total = jnp.dot(taps1[...], window, preferred_element_type=F32)
        for r in range(BAND):
            i = start + r
            half = total[r * channels : (r + 1) * channels] + bias1
            value = half + half * jnp.tanh(half)
            if left is not None and i < HALO - 1:
                value = value * left
            if right is not None and i >= rows - 2 - (HALO - 1):
                value = value * right
            second[i] = value.astype(BF16)
    split = reach * channels
    for parity in range(2):
        for group in groups_of(run // 2):
            start = 2 * group + parity
            near = [first[start + 1 + 2 * i] for i in range(reach)]
            far = [second[start + 2 * i] for i in range(reach)]
            total = jnp.dot(
                taps2[:, :split], jnp.concatenate(near, axis=0), preferred_element_type=F32
            ) + jnp.dot(taps2[:, split:], jnp.concatenate(far, axis=0), preferred_element_type=F32)
            for r in range(BAND):
                n = start + 2 * r
                half = total[r * channels : (r + 1) * channels] + bias2
                third = (half + half * jnp.tanh(half)).astype(BF16).astype(F32)
                rest = jnp.sum(third * last, axis=0, keepdims=True)
                at = BAND * channels + r
                heads[n : n + 1, :] = total[at : at + 1] + rest


def in_runs(ext):
    run = (ext.shape[0] - 2 * HALO) // PARTS
    return jnp.concatenate([ext[q * run : (q + 1) * run + 2 * HALO] for q in range(PARTS)], axis=1)


def split3(value):
    one = value.astype(BF16)
    rest = value - one.astype(F32)
    two = rest.astype(BF16)
    three = (rest - two.astype(F32)).astype(BF16)
    return jnp.concatenate([one, two, three], axis=1)


def blank_kernel(blank):
    blank[...] = jnp.zeros_like(blank)


def end_masks(parts, members):
    space = lax.axis_index("space")
    lane = lax.broadcasted_iota(jnp.int32, (1, parts * members), 1)
    left = (lane < members) & (space == 0)
    right = (lane >= (parts - 1) * members) & (space == lax.axis_size("space") - 1)
    return jnp.where(left, 0.0, 1.0), jnp.where(right, 0.0, 1.0)


def prepare_kernel(
    empty, field, gain, bias, conv1, bias1, conv2, bias2, readout,
    obs_heads, obs_var, noise_turned, obs_index, obs_count,
    own, taps1, taps2, columns, sent,
    wide1, wide2, first, second, heads,
):
    space = lax.axis_index("space")
    spaces = lax.axis_size("space")
    turned = field[...].T
    own[...] = turned
    cells, members = turned.shape
    channels = gain.shape[0]
    row = readout[...].astype(F32).reshape(1, 3 * channels)
    split = (BAND + 2) * channels
    wide1[...] = jnp.zeros_like(wide1)
    wide2[...] = jnp.zeros_like(wide2)
    for tap in range(3):
        one = 0.5 * conv1[tap].astype(F32)
        both = 0.5 * conv2[tap].astype(F32)
        for r in range(BAND):
            out = slice(r * channels, (r + 1) * channels)
            at = (r + tap) * channels
            wide1[out, at : at + channels] = one
            wide2[out, at : at + channels] = both[:, :channels]
            wide2[out, split + at : split + at + channels] = both[:, channels:]
    for r in range(BAND):
        out, at = BAND * channels + r, (r + 1) * channels
        wide2[out : out + 1, at : at + channels] = row[:, :channels]
        wide2[out : out + 1, split + at : split + at + channels] = row[:, channels : 2 * channels]
    taps1[...] = wide1[...].astype(BF16)
    taps2[...] = wide2[...].astype(BF16)
    rows = [
        gain[...].reshape(1, channels),
        bias[...].reshape(1, channels),
        0.5 * bias1[...].reshape(1, channels),
        0.5 * bias2[...].reshape(1, channels),
        row[:, 2 * channels :],
    ]
    for spot, value in enumerate(rows):
        columns[spot] = jnp.broadcast_to(column(value), (channels, columns.shape[2]))
    slots = obs_var.shape[0]
    cell = obs_index[...]
    low_end = (cell < HALO) & (space > 0)
    high_end = (cell >= cells - HALO) & (space < spaces - 1)
    end_row = jnp.where(
        low_end,
        (space - 1) * EDGE + HALO + cell,
        jnp.where(high_end, space * EDGE + cell - (cells - HALO), -1),
    )
    inside = column(jnp.where(end_row < 0, cell, -1).astype(F32)).astype(jnp.int32)
    chosen = jnp.where(
        lax.broadcasted_iota(jnp.int32, (slots, cells), 1) == inside, 1.0, 0.0
    ).astype(BF16)
    variance = obs_var[...].reshape(1, slots)
    live = lax.broadcasted_iota(jnp.int32, (1, slots), 1) < obs_count[...].reshape(1, 1)
    root_row = jnp.where(live, lax.rsqrt(variance), 0.0)
    root = column(root_row)
    target = column(obs_heads[...].reshape(1, slots))
    goal = root * target
    noise = jnp.where(column(jnp.where(live, 1.0, 0.0)) > 0.0, noise_turned[...], 0.0)

    zeros = jnp.zeros((HALO, members), F32)
    wide = in_runs(jnp.concatenate([zeros, turned, zeros], axis=0))
    left, right = end_masks(PARTS, members)
    layers(wide, cells // PARTS, left, right, taps1, taps2, columns, first, second, heads)
    every = jnp.concatenate(
        [heads[:, q * members : (q + 1) * members] for q in range(PARTS)], axis=0
    )
    parts = jnp.dot(chosen, split3(every), preferred_element_type=F32)
    seen = parts[:, :members] + parts[:, members : 2 * members] + parts[:, 2 * members :]
    gap = goal - root * seen
    gap_high = gap.astype(BF16).astype(F32)
    root_high = root_row.astype(BF16).astype(F32)
    ends = jnp.concatenate([turned[: 2 * HALO], turned[cells - 2 * HALO :]], axis=1)
    ends_high = ends.astype(BF16).astype(F32)
    row_high = (end_row >> 6) << 6
    blank = empty[0:1, slots : 2 * members]
    payload = jnp.concatenate(
        [
            jnp.concatenate([gap_high, gap - gap_high], axis=1),
            jnp.concatenate([noise[: slots // 2], noise[slots // 2 :]], axis=1),
            ends_high,
            jnp.concatenate([row_high.astype(F32), blank], axis=1),
            jnp.concatenate([root_high, blank], axis=1),
            ends - ends_high,
            jnp.concatenate([(end_row - row_high).astype(F32), blank], axis=1),
            jnp.concatenate([root_row - root_high, blank], axis=1),
        ],
        axis=0,
    ).astype(BF16)
    for copy in range(sent.shape[0]):
        sent[copy] = payload


def tables_kernel(neighbours, near, near_turned, choice):
    members, order = neighbours.shape
    everyone = choice.shape[2]
    ids = neighbours[...] - members * lax.axis_index("members")
    ids = jnp.where(ids < 0, ids + everyone, ids)
    pair = jnp.concatenate([ids, ids], axis=1)
    table = jnp.concatenate([pair, pair], axis=0)
    near[...] = table
    turned = pair.T[:order]
    near_turned[...] = jnp.concatenate([turned, turned], axis=1)
    second_half = (lax.broadcasted_iota(jnp.int32, (128, 128), 0) >= 64).astype(jnp.int32)
    everyone_id = lax.broadcasted_iota(jnp.int32, (128, everyone), 1)
    for two in range(order // 2):
        member = jnp.take_along_axis(
            table, 2 * two + second_half, axis=1, mode="promise_in_bounds"
        )
        member = jnp.concatenate([member] * (everyone // 128), axis=1)
        choice[two] = jnp.where(member == everyone_id, 1.0, 0.0).astype(BF16)


def ends_kernel(
    got, own, taps1, taps2, columns,
    kept, swapped, first, second, heads, ends, marks, tails,
):
    space = lax.axis_index("space")
    spaces = got.shape[0]
    slots = (got.shape[1] - 2 * EDGE) * 2 // 3
    members = got.shape[2] // 2
    inner = 2 * HALO
    edge = slots + slots // 2
    for tile in range(spaces):
        pair = got[tile].astype(F32)[edge:]
        tails[tile] = pair[:EDGE] + pair[EDGE:]
    for start in range(0, spaces, PARTS):
        sides = []
        for here in range(start, start + PARTS):
            there = (here + 1) % spaces
            near_end = tails[here, :inner, members:]
            far_end = tails[there, :inner, :members]
            sides.append(jnp.concatenate([near_end, far_end], axis=0))
        wide = jnp.concatenate(sides, axis=1)
        turn = start // PARTS
        layers(
            wide, inner, None, None, taps1, taps2, columns,
            first.at[turn], second.at[turn], heads.at[turn],
        )
        for q in range(PARTS):
            at = (start + q) * EDGE
            ends[at : at + EDGE, :] = heads[turn, :, q * members : (q + 1) * members]
    for tile in range(spaces):
        at = tile * slots
        marks[0:2, at : at + slots] = tails[tile, inner : inner + 2, :slots]
    row = lax.broadcasted_iota(jnp.int32, (spaces * EDGE, spaces * slots), 0).astype(F32)
    picks = jnp.where(row == marks[0:1, :], marks[1:2, :], 0.0)
    added = lax.dot_general(
        picks, jnp.concatenate([ends[...]] * 2, axis=1), (((0,), (0,)), ((), ())),
        precision=lax.Precision.HIGHEST, preferred_element_type=F32,
    )
    heads_lane = lax.broadcasted_iota(jnp.int32, (1, 2 * members), 1) < members
    half = spaces * slots // 2

    def finished(tile):
        at = slice(tile * slots, (tile + 1) * slots)
        there = got[tile].astype(F32)
        gap = there[:slots] + pltpu.roll(there[:slots], members, 1) - added[at]
        noise = there[slots:edge]
        noise = jnp.concatenate([pltpu.roll(noise, members, 1), noise], axis=0)
        return jnp.where(heads_lane, gap, gap + noise)

    for tile in range(spaces // 2):
        at = slice(tile * slots, (tile + 1) * slots)
        one, two = finished(tile), finished(tile + spaces // 2)
        kept[at, :] = one
        kept[half + tile * slots : half + (tile + 1) * slots, :] = two
        swapped[at, :] = jnp.where(heads_lane, one, pltpu.roll(two, members, 1))
    before = jnp.where(space == 0, spaces - 1, space - 1)
    after = jnp.where(space == spaces - 1, 0, space + 1)
    swapped[half : half + EDGE, :] = tails[before]
    swapped[half + EDGE : half + 2 * EDGE, :] = tails[after]
    middle = own.shape[0] // 2
    swapped[half + 2 * EDGE :, :] = jnp.concatenate([own[:middle, :], own[middle:, :]], axis=1)


def lane_gather(table, index):
    low = index & 127
    high = index >> 7
    found = None
    for tile in range(table.shape[1] // 128):
        part = jnp.take_along_axis(
            table[:, tile * 128 : (tile + 1) * 128], low, axis=1, mode="promise_in_bounds"
        )
        found = part if found is None else jnp.where(high == tile, part, found)
    return found


def update_kernel(groups, *refs):
    kept, parcels = refs[0], refs[1 : 1 + groups]
    (
        taps1, taps2, columns, near, near_turned, choice,
        updated, new_heads,
        system, first, second, heads, turned,
    ) = refs[1 + groups :]
    cells = updated.shape[1]
    slots, members = kept.shape[0], kept.shape[1] // 2
    everyone = groups * members
    order = near.shape[0] // 2
    half_lane = lax.broadcasted_iota(jnp.int32, (1, 128), 1) < 64

    panel = []
    for g in range(0, groups, 2):
        right = parcels[g + 1][0 : slots // 2, :]
        right = jnp.concatenate([pltpu.roll(right, members, 1), right], axis=0)
        if g:
            left = parcels[g][0 : slots // 2, :]
            left = jnp.concatenate([left, pltpu.roll(left, members, 1)], axis=0)
        else:
            left = kept[...]
        panel.append(jnp.where(half_lane, left, right))
    panel = jnp.concatenate(panel, axis=1)
    panel = panel - jnp.mean(panel, axis=1, keepdims=True)
    innovation = kept[:, members:]
    stacked = jnp.concatenate([panel, innovation], axis=1)
    product = lax.dot_general(
        stacked, panel, (((0,), (0,)), ((), ())),
        precision=lax.Precision.HIGHEST, preferred_element_type=F32,
    )
    gram = split3(product[:everyone])
    sides = -product[everyone:]

    ids = near[...]
    lane_id = lax.broadcasted_iota(jnp.int32, (128, 128), 1)
    row_id = lax.broadcasted_iota(jnp.int32, (128, 128), 0)

    def extract(quad, carry):
        found = []
        for b in range(2):
            parts = jnp.dot(choice[2 * quad + b], gram, preferred_element_type=F32)
            rows = (
                parts[:, :everyone]
                + parts[:, everyone : 2 * everyone]
                + parts[:, 2 * everyone :]
            )
            found.append(lane_gather(rows, ids))
        block = jnp.where(half_lane, found[0], found[1]).T
        own = 4 * quad + 2 * (row_id >= 64).astype(jnp.int32) + (lane_id >= 64).astype(jnp.int32)
        block = block + jnp.where((row_id & 63) == own, order - 1.0, 0.0)
        system[pl.ds(pl.multiple_of(quad * 128, 128), 128), :] = block
        return carry

    lax.fori_loop(0, order // 4, extract, 0, unroll=order // 4)
    side = lane_gather(jnp.concatenate([sides, sides], axis=0), ids)
    side = jnp.where(row_id >= 64, 1.0, side).T[:order]
    system[order // 2 * order : (order // 2 + 1) * order, :] = side

    blocks = order // 2
    def both(value):
        turn = pltpu.roll(value, 64, 1)
        return jnp.where(half_lane, value, turn), jnp.where(half_lane, turn, value)

    def without(value, pair):
        at = 2 * pair // 8 * 8
        row = lax.broadcasted_iota(jnp.int32, (8, 128), 0) + at
        tile = jnp.where((row >= 2 * pair) & (row < 2 * pair + 2), 0.0, value[at : at + 8])
        parts = [value[:at], tile, value[at + 8 :]]
        return jnp.concatenate([part for part in parts if part.shape[0]], axis=0)

    def factors(col0, col1, pair):
        one, two = 2 * pair, 2 * pair + 1
        d, e, f = col0[one:two], col1[one:two], col1[two : two + 1]
        inv = 1.0 / (d * f - e * e)
        fac0 = without((col0 * f - col1 * e) * inv, pair)
        fac1 = without((col1 * d - col0 * e) * inv, pair)
        return fac0, fac1, (f * inv, d * inv, e * inv)

    own_share, cross_share = [], []
    fac0, fac1, shares = factors(*both(system[0:order, :]), 0)
    for pair in range(blocks):
        own_share += [shares[0], shares[1]]
        cross_share += [shares[2], shares[2]]
        one, two = 2 * pair, 2 * pair + 1
        if pair + 1 < blocks:
            col0, col1 = both(system[(pair + 1) * order : (pair + 2) * order, :])
            later = factors(
                col0 - fac0 * col0[one:two] - fac1 * col0[two : two + 1],
                col1 - fac0 * col1[one:two] - fac1 * col1[two : two + 1],
                pair + 1,
            )
        for block in range(min(pair + 2, blocks), blocks + 1):
            at = block * order
            row0 = system[at + one : at + two, :]
            row1 = system[at + two : at + two + 1, :]
            system[at : at + order, :] = system[at : at + order, :] - fac0 * row0 - fac1 * row1
        if pair + 1 < blocks:
            fac0, fac1, shares = later
    sides = system[blocks * order :, :]
    even = lax.broadcasted_iota(jnp.int32, (order, 128), 0) % 2 == 0
    partner = jnp.where(even, pltpu.roll(sides, order - 1, 0), pltpu.roll(sides, 1, 0))
    solved = sides * jnp.concatenate(own_share, axis=0) - partner * jnp.concatenate(
        cross_share, axis=0
    )
    sums = jnp.sum(solved, axis=0, keepdims=True)
    share = sums / pltpu.roll(sums, 64, 1)
    coef = (solved - pltpu.roll(solved, 64, 1) * share)[:, :members]
    coef = coef - jnp.mean(coef, axis=0, keepdims=True)
    coef = jnp.concatenate([coef, coef], axis=1)
    name = lax.broadcasted_iota(jnp.int32, (everyone // 2, 128), 0) + jnp.where(
        half_lane, 0, everyone // 2
    )
    mixing = jnp.zeros((everyone // 2, 128), F32)
    for i in range(order):
        mixing = jnp.where(name == near_turned[i : i + 1, :], coef[i : i + 1], mixing)
    mixing = jnp.concatenate([mixing[:, :members], mixing[:, members:]], axis=0)

    before = slots // 2
    after, body = before + EDGE, before + 2 * EDGE
    sources = jnp.concatenate(
        [
            jnp.concatenate([full[before + HALO : before + 2 * HALO, members:] for full in parcels], axis=1),
            jnp.concatenate([full[body:, :members] for full in parcels], axis=1),
            jnp.concatenate([full[body:, members:] for full in parcels], axis=1),
            jnp.concatenate([full[after : after + HALO, :members] for full in parcels], axis=1),
        ],
        axis=0,
    )
    field = sources[:, :members] + jnp.dot(
        sources, mixing, precision=lax.Precision.HIGHEST, preferred_element_type=F32
    )
    updated[...] = field[HALO : HALO + cells].T
    run = cells // PARTS
    left, right = end_masks(PARTS, members)
    layers(in_runs(field), run, left, right, taps1, taps2, columns, first, second, heads)
    for q in range(PARTS):
        turned[q * run : (q + 1) * run, :] = heads[:, q * members : (q + 1) * members]
    new_heads[...] = turned[...].T


def from_groups(value):
    groups = lax.axis_size("members")
    found = [value]
    for step in range(1, groups):
        pairs = [((i + step) % groups, i) for i in range(groups)]
        found.append(lax.ppermute(value, "members", pairs))
    return found


def on_device(
    log_field, obs_heads, obs_var, obs_noise, obs_index, obs_count, neighbours,
    lift_gain, lift_bias, conv_first, bias_first, conv_second, bias_second, readout,
):
    members, cells = log_field.shape
    spaces = lax.axis_size("space")
    groups = lax.axis_size("members")
    channels = lift_gain.shape[0]
    slots = obs_var.shape[0]
    order = neighbours.shape[1]

    def work(run, parts):
        rows, lanes = run + 2 * HALO, parts * members
        return (
            pltpu.VMEM((rows, channels, lanes), BF16),
            pltpu.VMEM((rows - 2, channels, lanes), BF16),
            pltpu.VMEM((max(run, 8), lanes), F32),
        )

    reach = (BAND + 2) * channels
    empty = call(blank_kernel, shape((8, 2 * members)), (), flops=1 << 34)
    own, taps1, taps2, columns, sent = call(
        prepare_kernel,
        (
            shape((cells, members)),
            shape((BAND * channels, reach), BF16),
            shape((BAND * channels + 16, 2 * reach), BF16),
            shape((5, channels, 128)),
            shape((spaces, slots + slots // 2 + 2 * EDGE, 2 * members), BF16),
        ),
        (
            empty, log_field, lift_gain, lift_bias, conv_first, bias_first, conv_second, bias_second,
            readout, obs_heads, obs_var, obs_noise.T, obs_index, obs_count,
        ),
        scratch=(
            pltpu.VMEM((BAND * channels, reach), F32),
            pltpu.VMEM((BAND * channels + 16, 2 * reach), F32),
        )
        + work(cells // PARTS, PARTS),
    )
    got = lax.all_to_all(sent, "space", 0, 0)
    near, near_turned, choice = call(
        tables_kernel,
        (
            shape((2 * members, 2 * order), jnp.int32),
            shape((order, 2 * members), jnp.int32),
            shape((order // 2, 2 * members, groups * members), BF16),
        ),
        (neighbours,),
        flops=1 << 30,
    )
    turns = spaces // PARTS
    kept, swapped = call(
        ends_kernel,
        (
            shape((spaces * slots, 2 * members)),
            shape((spaces * slots // 2 + 2 * EDGE + cells // 2, 2 * members)),
        ),
        (got, own, taps1, taps2, columns),
        scratch=tuple(
            pltpu.VMEM((turns, *value.shape), value.dtype) for value in work(2 * HALO, PARTS)
        )
        + (
            pltpu.VMEM((spaces * EDGE, members), F32),
            pltpu.VMEM((8, spaces * slots), F32),
            pltpu.VMEM((spaces, EDGE, 2 * members), F32),
        ),
    )
    return call(
        functools.partial(update_kernel, groups),
        (shape((members, cells)), shape((members, cells))),
        (kept, *from_groups(swapped), taps1, taps2, columns, near, near_turned, choice),
        scratch=(pltpu.VMEM(((order // 2 + 1) * order, 128), F32),)
        + work(cells // PARTS, PARTS)
        + (pltpu.VMEM((cells, members), F32),),
    )


def solution(mesh):
    in_specs = (
        P("members", "space"),
        P("space"),
        P("space"),
        P("members", "space"),
        P("space", None),
        P("space"),
        P("members", None),
        P(),
        P(),
        P(),
        P(),
        P(),
        P(),
        P(),
    )
    out_specs = (P("members", "space"), P("members", "space"))
    return jax.shard_map(
        on_device, mesh=mesh, in_specs=in_specs, out_specs=out_specs, check_vma=False
    )
```

```python
import functools

import jax
import jax.numpy as jnp
from jax import lax
from jax.experimental import pallas as pl
from jax.experimental.pallas import tpu as pltpu
from jax.sharding import PartitionSpec as P

F32 = jnp.float32
BF16 = jnp.bfloat16
HALO = 3
EDGE = 8
PARTS = 4
BAND = 3
VMEM = pl.BlockSpec(memory_space=pltpu.VMEM)


def shape(dims, dtype=F32):
    return jax.ShapeDtypeStruct(dims, dtype)


def call(kernel, outs, args, scratch=(), flops=0, limit=40):
    return pl.pallas_call(
        kernel,
        out_shape=outs,
        in_specs=[VMEM] * len(args),
        out_specs=jax.tree.map(lambda _: VMEM, outs),
        scratch_shapes=list(scratch),
        cost_estimate=pl.CostEstimate(flops=flops, bytes_accessed=1 << 18, transcendentals=0),
        compiler_params=pltpu.CompilerParams(vmem_limit_bytes=limit << 20),
    )(*args)


def column(row):
    size = row.shape[1]
    same = lax.broadcasted_iota(jnp.int32, (size, size), 0) == lax.broadcasted_iota(
        jnp.int32, (size, size), 1
    )
    return jnp.sum(jnp.where(same, row, 0.0), axis=1, keepdims=True)


def groups_of(count):
    return [min(at, count - BAND) for at in range(0, count, BAND)]


def layers(wide, run, left, right, taps1, taps2, columns, first, second, heads):
    lanes = wide.shape[1]
    rows = run + 2 * HALO
    gain, bias, bias1, bias2, last = [
        jnp.concatenate([columns[i]] * (lanes // columns.shape[2]), axis=1) for i in range(5)
    ]
    channels = gain.shape[0]
    for r in range(rows):
        value = jnp.tanh(gain * wide[r : r + 1] + bias)
        if left is not None and r < HALO:
            value = value * left
        if right is not None and r >= rows - HALO:
            value = value * right
        first[r] = value.astype(BF16)
    reach = BAND + 2
    for start in groups_of(rows - 2):
        window = first[start : start + reach].reshape(reach * channels, lanes)
        total = jnp.dot(taps1[...], window, preferred_element_type=F32)
        for r in range(BAND):
            i = start + r
            half = total[r * channels : (r + 1) * channels] + bias1
            value = half + half * jnp.tanh(half)
            if left is not None and i < HALO - 1:
                value = value * left
            if right is not None and i >= rows - 2 - (HALO - 1):
                value = value * right
            second[i] = value.astype(BF16)
    split = reach * channels
    for parity in range(2):
        for group in groups_of(run // 2):
            start = 2 * group + parity
            near = [first[start + 1 + 2 * i] for i in range(reach)]
            far = [second[start + 2 * i] for i in range(reach)]
            total = jnp.dot(
                taps2[:, :split], jnp.concatenate(near, axis=0), preferred_element_type=F32
            ) + jnp.dot(taps2[:, split:], jnp.concatenate(far, axis=0), preferred_element_type=F32)
            for r in range(BAND):
                n = start + 2 * r
                half = total[r * channels : (r + 1) * channels] + bias2
                third = (half + half * jnp.tanh(half)).astype(BF16).astype(F32)
                rest = jnp.sum(third * last, axis=0, keepdims=True)
                at = BAND * channels + r
                heads[n : n + 1, :] = total[at : at + 1] + rest


def in_runs(ext):
    run = (ext.shape[0] - 2 * HALO) // PARTS
    return jnp.concatenate([ext[q * run : (q + 1) * run + 2 * HALO] for q in range(PARTS)], axis=1)


def split3(value):
    one = value.astype(BF16)
    rest = value - one.astype(F32)
    two = rest.astype(BF16)
    three = (rest - two.astype(F32)).astype(BF16)
    return jnp.concatenate([one, two, three], axis=1)


def blank_kernel(blank):
    blank[...] = jnp.zeros_like(blank)


def end_masks(parts, members):
    space = lax.axis_index("space")
    lane = lax.broadcasted_iota(jnp.int32, (1, parts * members), 1)
    left = (lane < members) & (space == 0)
    right = (lane >= (parts - 1) * members) & (space == lax.axis_size("space") - 1)
    return jnp.where(left, 0.0, 1.0), jnp.where(right, 0.0, 1.0)


def prepare_kernel(
    empty, field, gain, bias, conv1, bias1, conv2, bias2, readout,
    obs_heads, obs_var, noise_turned, obs_index, obs_count,
    own, taps1, taps2, columns, sent,
    wide1, wide2, first, second, heads,
):
    space = lax.axis_index("space")
    spaces = lax.axis_size("space")
    turned = field[...].T
    own[...] = turned
    cells, members = turned.shape
    channels = gain.shape[0]
    row = readout[...].astype(F32).reshape(1, 3 * channels)
    split = (BAND + 2) * channels
    wide1[...] = jnp.zeros_like(wide1)
    wide2[...] = jnp.zeros_like(wide2)
    for tap in range(3):
        one = 0.5 * conv1[tap].astype(F32)
        both = 0.5 * conv2[tap].astype(F32)
        for r in range(BAND):
            out = slice(r * channels, (r + 1) * channels)
            at = (r + tap) * channels
            wide1[out, at : at + channels] = one
            wide2[out, at : at + channels] = both[:, :channels]
            wide2[out, split + at : split + at + channels] = both[:, channels:]
    for r in range(BAND):
        out, at = BAND * channels + r, (r + 1) * channels
        wide2[out : out + 1, at : at + channels] = row[:, :channels]
        wide2[out : out + 1, split + at : split + at + channels] = row[:, channels : 2 * channels]
    taps1[...] = wide1[...].astype(BF16)
    taps2[...] = wide2[...].astype(BF16)
    rows = [
        gain[...].reshape(1, channels),
        bias[...].reshape(1, channels),
        0.5 * bias1[...].reshape(1, channels),
        0.5 * bias2[...].reshape(1, channels),
        row[:, 2 * channels :],
    ]
    for spot, value in enumerate(rows):
        columns[spot] = jnp.broadcast_to(column(value), (channels, columns.shape[2]))
    slots = obs_var.shape[0]
    cell = obs_index[...]
    low_end = (cell < HALO) & (space > 0)
    high_end = (cell >= cells - HALO) & (space < spaces - 1)
    end_row = jnp.where(
        low_end,
        (space - 1) * EDGE + HALO + cell,
        jnp.where(high_end, space * EDGE + cell - (cells - HALO), -1),
    )
    inside = column(jnp.where(end_row < 0, cell, -1).astype(F32)).astype(jnp.int32)
    chosen = jnp.where(
        lax.broadcasted_iota(jnp.int32, (slots, cells), 1) == inside, 1.0, 0.0
    ).astype(BF16)
    variance = obs_var[...].reshape(1, slots)
    live = lax.broadcasted_iota(jnp.int32, (1, slots), 1) < obs_count[...].reshape(1, 1)
    root_row = jnp.where(live, lax.rsqrt(variance), 0.0)
    root = column(root_row)
    target = column(obs_heads[...].reshape(1, slots))
    goal = root * target
    noise = jnp.where(column(jnp.where(live, 1.0, 0.0)) > 0.0, noise_turned[...], 0.0)

    zeros = jnp.zeros((HALO, members), F32)
    wide = in_runs(jnp.concatenate([zeros, turned, zeros], axis=0))
    left, right = end_masks(PARTS, members)
    layers(wide, cells // PARTS, left, right, taps1, taps2, columns, first, second, heads)
    every = jnp.concatenate(
        [heads[:, q * members : (q + 1) * members] for q in range(PARTS)], axis=0
    )
    parts = jnp.dot(chosen, split3(every), preferred_element_type=F32)
    seen = parts[:, :members] + parts[:, members : 2 * members] + parts[:, 2 * members :]
    gap = goal - root * seen
    gap_high = gap.astype(BF16).astype(F32)
    root_high = root_row.astype(BF16).astype(F32)
    ends = jnp.concatenate([turned[: 2 * HALO], turned[cells - 2 * HALO :]], axis=1)
    ends_high = ends.astype(BF16).astype(F32)
    row_high = (end_row >> 6) << 6
    blank = empty[0:1, slots : 2 * members]
    payload = jnp.concatenate(
        [
            jnp.concatenate([gap_high, gap - gap_high], axis=1),
            jnp.concatenate([noise[: slots // 2], noise[slots // 2 :]], axis=1),
            ends_high,
            jnp.concatenate([row_high.astype(F32), blank], axis=1),
            jnp.concatenate([root_high, blank], axis=1),
            ends - ends_high,
            jnp.concatenate([(end_row - row_high).astype(F32), blank], axis=1),
            jnp.concatenate([root_row - root_high, blank], axis=1),
        ],
        axis=0,
    ).astype(BF16)
    for copy in range(sent.shape[0]):
        sent[copy] = payload


def tables_kernel(neighbours, near, near_turned, choice):
    members, order = neighbours.shape
    everyone = choice.shape[2]
    ids = neighbours[...] - members * lax.axis_index("members")
    ids = jnp.where(ids < 0, ids + everyone, ids)
    pair = jnp.concatenate([ids, ids], axis=1)
    table = jnp.concatenate([pair, pair], axis=0)
    near[...] = table
    turned = pair.T[:order]
    near_turned[...] = jnp.concatenate([turned, turned], axis=1)
    second_half = (lax.broadcasted_iota(jnp.int32, (128, 128), 0) >= 64).astype(jnp.int32)
    everyone_id = lax.broadcasted_iota(jnp.int32, (128, everyone), 1)
    for two in range(order // 2):
        member = jnp.take_along_axis(
            table, 2 * two + second_half, axis=1, mode="promise_in_bounds"
        )
        member = jnp.concatenate([member] * (everyone // 128), axis=1)
        choice[two] = jnp.where(member == everyone_id, 1.0, 0.0).astype(BF16)


def ends_kernel(
    got, own, taps1, taps2, columns,
    kept, swapped, first, second, heads, ends, marks, tails,
):
    space = lax.axis_index("space")
    spaces = got.shape[0]
    slots = (got.shape[1] - 2 * EDGE) * 2 // 3
    members = got.shape[2] // 2
    inner = 2 * HALO
    edge = slots + slots // 2
    for tile in range(spaces):
        pair = got[tile].astype(F32)[edge:]
        tails[tile] = pair[:EDGE] + pair[EDGE:]
    ends[...] = jnp.zeros_like(ends)
    for start in range(0, spaces, PARTS):
        sides = []
        for here in range(start, start + PARTS):
            there = (here + 1) % spaces
            near_end = tails[here, :inner, members:]
            far_end = tails[there, :inner, :members]
            sides.append(jnp.concatenate([near_end, far_end], axis=0))
        wide = jnp.concatenate(sides, axis=1)
        turn = start // PARTS
        layers(
            wide, inner, None, None, taps1, taps2, columns,
            first.at[turn], second.at[turn], heads.at[turn],
        )
        for q in range(PARTS):
            at = (start + q) * EDGE
            ends[at : at + inner, :] = heads[turn, :inner, q * members : (q + 1) * members]
    for tile in range(spaces):
        at = tile * slots
        marks[0:2, at : at + slots] = tails[tile, inner : inner + 2, :slots]
    row = lax.broadcasted_iota(jnp.int32, (spaces * EDGE, spaces * slots), 0).astype(F32)
    picks = jnp.where(row == marks[0:1, :], marks[1:2, :], 0.0)
    added = lax.dot_general(
        picks, jnp.concatenate([ends[...]] * 2, axis=1), (((0,), (0,)), ((), ())),
        precision=lax.Precision.HIGHEST, preferred_element_type=F32,
    )
    heads_lane = lax.broadcasted_iota(jnp.int32, (1, 2 * members), 1) < members
    half = spaces * slots // 2

    def finished(tile):
        at = slice(tile * slots, (tile + 1) * slots)
        there = got[tile].astype(F32)
        gap = there[:slots] + pltpu.roll(there[:slots], members, 1) - added[at]
        noise = there[slots:edge]
        noise = jnp.concatenate([pltpu.roll(noise, members, 1), noise], axis=0)
        return jnp.where(heads_lane, gap, gap + noise)

    for tile in range(spaces // 2):
        at = slice(tile * slots, (tile + 1) * slots)
        one, two = finished(tile), finished(tile + spaces // 2)
        kept[at, :] = one
        kept[half + tile * slots : half + (tile + 1) * slots, :] = two
        swapped[at, :] = jnp.where(heads_lane, one, pltpu.roll(two, members, 1))
    before = jnp.where(space == 0, spaces - 1, space - 1)
    after = jnp.where(space == spaces - 1, 0, space + 1)
    swapped[half : half + EDGE, :] = tails[before]
    swapped[half + EDGE : half + 2 * EDGE, :] = tails[after]
    middle = own.shape[0] // 2
    swapped[half + 2 * EDGE :, :] = jnp.concatenate([own[:middle, :], own[middle:, :]], axis=1)


def lane_gather(table, index):
    low = index & 127
    high = index >> 7
    found = None
    for tile in range(table.shape[1] // 128):
        part = jnp.take_along_axis(
            table[:, tile * 128 : (tile + 1) * 128], low, axis=1, mode="promise_in_bounds"
        )
        found = part if found is None else jnp.where(high == tile, part, found)
    return found


def update_kernel(groups, *refs):
    kept, parcels = refs[0], refs[1 : 1 + groups]
    (
        taps1, taps2, columns, near, near_turned, choice,
        updated, new_heads,
        system, first, second, heads, turned,
    ) = refs[1 + groups :]
    cells = updated.shape[1]
    slots, members = kept.shape[0], kept.shape[1] // 2
    everyone = groups * members
    order = near.shape[0] // 2
    half_lane = lax.broadcasted_iota(jnp.int32, (1, 128), 1) < 64

    panel = []
    for g in range(0, groups, 2):
        right = parcels[g + 1][0 : slots // 2, :]
        right = jnp.concatenate([pltpu.roll(right, members, 1), right], axis=0)
        if g:
            left = parcels[g][0 : slots // 2, :]
            left = jnp.concatenate([left, pltpu.roll(left, members, 1)], axis=0)
        else:
            left = kept[...]
        panel.append(jnp.where(half_lane, left, right))
    panel = jnp.concatenate(panel, axis=1)
    panel = panel - jnp.mean(panel, axis=1, keepdims=True)
    innovation = kept[:, members:]
    stacked = jnp.concatenate([panel, innovation], axis=1)
    product = lax.dot_general(
        stacked, panel, (((0,), (0,)), ((), ())),
        precision=lax.Precision.HIGHEST, preferred_element_type=F32,
    )
    gram = split3(product[:everyone])
    sides = -product[everyone:]

    ids = near[...]
    lane_id = lax.broadcasted_iota(jnp.int32, (128, 128), 1)
    row_id = lax.broadcasted_iota(jnp.int32, (128, 128), 0)

    def extract(quad, carry):
        found = []
        for b in range(2):
            parts = jnp.dot(choice[2 * quad + b], gram, preferred_element_type=F32)
            rows = (
                parts[:, :everyone]
                + parts[:, everyone : 2 * everyone]
                + parts[:, 2 * everyone :]
            )
            found.append(lane_gather(rows, ids))
        block = jnp.where(half_lane, found[0], found[1]).T
        own = 4 * quad + 2 * (row_id >= 64).astype(jnp.int32) + (lane_id >= 64).astype(jnp.int32)
        block = block + jnp.where((row_id & 63) == own, order - 1.0, 0.0)
        system[pl.ds(pl.multiple_of(quad * 128, 128), 128), :] = block
        return carry

    lax.fori_loop(0, order // 4, extract, 0, unroll=order // 4)
    side = lane_gather(jnp.concatenate([sides, sides], axis=0), ids)
    side = jnp.where(row_id >= 64, 1.0, side).T[:order]
    system[order // 2 * order : (order // 2 + 1) * order, :] = side

    blocks = order // 2
    def both(value):
        turn = pltpu.roll(value, 64, 1)
        return jnp.where(half_lane, value, turn), jnp.where(half_lane, turn, value)

    def without(value, pair):
        at = 2 * pair // 8 * 8
        row = lax.broadcasted_iota(jnp.int32, (8, 128), 0) + at
        tile = jnp.where((row >= 2 * pair) & (row < 2 * pair + 2), 0.0, value[at : at + 8])
        parts = [value[:at], tile, value[at + 8 :]]
        return jnp.concatenate([part for part in parts if part.shape[0]], axis=0)

    def factors(col0, col1, pair):
        one, two = 2 * pair, 2 * pair + 1
        d, e, f = col0[one:two], col1[one:two], col1[two : two + 1]
        inv = 1.0 / (d * f - e * e)
        fac0 = without((col0 * f - col1 * e) * inv, pair)
        fac1 = without((col1 * d - col0 * e) * inv, pair)
        return fac0, fac1, (f * inv, d * inv, e * inv)

    own_share, cross_share = [], []
    fac0, fac1, shares = factors(*both(system[0:order, :]), 0)
    for pair in range(blocks):
        own_share += [shares[0], shares[1]]
        cross_share += [shares[2], shares[2]]
        one, two = 2 * pair, 2 * pair + 1
        if pair + 1 < blocks:
            col0, col1 = both(system[(pair + 1) * order : (pair + 2) * order, :])
            later = factors(
                col0 - fac0 * col0[one:two] - fac1 * col0[two : two + 1],
                col1 - fac0 * col1[one:two] - fac1 * col1[two : two + 1],
                pair + 1,
            )
        for block in range(min(pair + 2, blocks), blocks + 1):
            at = block * order
            row0 = system[at + one : at + two, :]
            row1 = system[at + two : at + two + 1, :]
            system[at : at + order, :] = system[at : at + order, :] - fac0 * row0 - fac1 * row1
        if pair + 1 < blocks:
            fac0, fac1, shares = later
    sides = system[blocks * order :, :]
    even = lax.broadcasted_iota(jnp.int32, (order, 128), 0) % 2 == 0
    partner = jnp.where(even, pltpu.roll(sides, order - 1, 0), pltpu.roll(sides, 1, 0))
    solved = sides * jnp.concatenate(own_share, axis=0) - partner * jnp.concatenate(
        cross_share, axis=0
    )
    sums = jnp.sum(solved, axis=0, keepdims=True)
    share = sums / pltpu.roll(sums, 64, 1)
    coef = (solved - pltpu.roll(solved, 64, 1) * share)[:, :members]
    coef = coef - jnp.mean(coef, axis=0, keepdims=True)
    coef = jnp.concatenate([coef, coef], axis=1)
    name = lax.broadcasted_iota(jnp.int32, (everyone // 2, 128), 0) + jnp.where(
        half_lane, 0, everyone // 2
    )
    mixing = jnp.zeros((everyone // 2, 128), F32)
    for i in range(order):
        mixing = jnp.where(name == near_turned[i : i + 1, :], coef[i : i + 1], mixing)
    mixing = jnp.concatenate([mixing[:, :members], mixing[:, members:]], axis=0)

    before = slots // 2
    after, body = before + EDGE, before + 2 * EDGE
    sources = jnp.concatenate(
        [
            jnp.concatenate([full[before + HALO : before + 2 * HALO, members:] for full in parcels], axis=1),
            jnp.concatenate([full[body:, :members] for full in parcels], axis=1),
            jnp.concatenate([full[body:, members:] for full in parcels], axis=1),
            jnp.concatenate([full[after : after + HALO, :members] for full in parcels], axis=1),
        ],
        axis=0,
    )
    field = sources[:, :members] + jnp.dot(
        sources, mixing, precision=lax.Precision.HIGHEST, preferred_element_type=F32
    )
    updated[...] = field[HALO : HALO + cells].T
    run = cells // PARTS
    left, right = end_masks(PARTS, members)
    layers(in_runs(field), run, left, right, taps1, taps2, columns, first, second, heads)
    for q in range(PARTS):
        turned[q * run : (q + 1) * run, :] = heads[:, q * members : (q + 1) * members]
    new_heads[...] = turned[...].T


def from_groups(value):
    groups = lax.axis_size("members")
    found = [value]
    for step in range(1, groups):
        pairs = [((i + step) % groups, i) for i in range(groups)]
        found.append(lax.ppermute(value, "members", pairs))
    return found


def on_device(
    log_field, obs_heads, obs_var, obs_noise, obs_index, obs_count, neighbours,
    lift_gain, lift_bias, conv_first, bias_first, conv_second, bias_second, readout,
):
    members, cells = log_field.shape
    spaces = lax.axis_size("space")
    groups = lax.axis_size("members")
    channels = lift_gain.shape[0]
    slots = obs_var.shape[0]
    order = neighbours.shape[1]

    def work(run, parts):
        rows, lanes = run + 2 * HALO, parts * members
        return (
            pltpu.VMEM((rows, channels, lanes), BF16),
            pltpu.VMEM((rows - 2, channels, lanes), BF16),
            pltpu.VMEM((max(run, 8), lanes), F32),
        )

    reach = (BAND + 2) * channels
    empty = call(blank_kernel, shape((8, 2 * members)), (), flops=1 << 34)
    own, taps1, taps2, columns, sent = call(
        prepare_kernel,
        (
            shape((cells, members)),
            shape((BAND * channels, reach), BF16),
            shape((BAND * channels + 16, 2 * reach), BF16),
            shape((5, channels, 128)),
            shape((spaces, slots + slots // 2 + 2 * EDGE, 2 * members), BF16),
        ),
        (
            empty, log_field, lift_gain, lift_bias, conv_first, bias_first, conv_second, bias_second,
            readout, obs_heads, obs_var, obs_noise.T, obs_index, obs_count,
        ),
        scratch=(
            pltpu.VMEM((BAND * channels, reach), F32),
            pltpu.VMEM((BAND * channels + 16, 2 * reach), F32),
        )
        + work(cells // PARTS, PARTS),
    )
    got = lax.all_to_all(sent, "space", 0, 0)
    near, near_turned, choice = call(
        tables_kernel,
        (
            shape((2 * members, 2 * order), jnp.int32),
            shape((order, 2 * members), jnp.int32),
            shape((order // 2, 2 * members, groups * members), BF16),
        ),
        (neighbours,),
        flops=1 << 30,
    )
    turns = spaces // PARTS
    kept, swapped = call(
        ends_kernel,
        (
            shape((spaces * slots, 2 * members)),
            shape((spaces * slots // 2 + 2 * EDGE + cells // 2, 2 * members)),
        ),
        (got, own, taps1, taps2, columns),
        scratch=tuple(
            pltpu.VMEM((turns, *value.shape), value.dtype) for value in work(2 * HALO, PARTS)
        )
        + (
            pltpu.VMEM((spaces * EDGE, members), F32),
            pltpu.VMEM((8, spaces * slots), F32),
            pltpu.VMEM((spaces, EDGE, 2 * members), F32),
        ),
    )
    return call(
        functools.partial(update_kernel, groups),
        (shape((members, cells)), shape((members, cells))),
        (kept, *from_groups(swapped), taps1, taps2, columns, near, near_turned, choice),
        scratch=(pltpu.VMEM(((order // 2 + 1) * order, 128), F32),)
        + work(cells // PARTS, PARTS)
        + (pltpu.VMEM((cells, members), F32),),
    )


def solution(mesh):
    in_specs = (
        P("members", "space"),
        P("space"),
        P("space"),
        P("members", "space"),
        P("space", None),
        P("space"),
        P("members", None),
        P(),
        P(),
        P(),
        P(),
        P(),
        P(),
        P(),
    )
    out_specs = (P("members", "space"), P("members", "space"))
    return jax.shard_map(
        on_device, mesh=mesh, in_specs=in_specs, out_specs=out_specs, check_vma=False
    )
```

```python
import functools

import jax
import jax.numpy as jnp
from jax import lax
from jax.experimental import pallas as pl
from jax.experimental.pallas import tpu as pltpu
from jax.sharding import PartitionSpec as P

F32 = jnp.float32
BF16 = jnp.bfloat16
HALO = 3
EDGE = 8
PARTS = 4
BAND = 3
VMEM = pl.BlockSpec(memory_space=pltpu.VMEM)


def shape(dims, dtype=F32):
    return jax.ShapeDtypeStruct(dims, dtype)


def call(kernel, outs, args, scratch=(), flops=0, limit=40):
    return pl.pallas_call(
        kernel,
        out_shape=outs,
        in_specs=[VMEM] * len(args),
        out_specs=jax.tree.map(lambda _: VMEM, outs),
        scratch_shapes=list(scratch),
        cost_estimate=pl.CostEstimate(flops=flops, bytes_accessed=1 << 18, transcendentals=0),
        compiler_params=pltpu.CompilerParams(vmem_limit_bytes=limit << 20),
    )(*args)


def column(row):
    size = row.shape[1]
    same = lax.broadcasted_iota(jnp.int32, (size, size), 0) == lax.broadcasted_iota(
        jnp.int32, (size, size), 1
    )
    return jnp.sum(jnp.where(same, row, 0.0), axis=1, keepdims=True)


def groups_of(count):
    return [min(at, count - BAND) for at in range(0, count, BAND)]


def layers(wide, run, left, right, taps1, taps2, columns, first, second, heads):
    lanes = wide.shape[1]
    rows = run + 2 * HALO
    gain, bias, bias1, bias2, last = [
        jnp.concatenate([columns[i]] * (lanes // columns.shape[2]), axis=1) for i in range(5)
    ]
    channels = gain.shape[0]
    for r in range(rows):
        value = jnp.tanh(gain * wide[r : r + 1] + bias)
        if left is not None and r < HALO:
            value = value * left
        if right is not None and r >= rows - HALO:
            value = value * right
        first[r] = value.astype(BF16)
    reach = BAND + 2
    for start in groups_of(rows - 2):
        window = first[start : start + reach].reshape(reach * channels, lanes)
        total = jnp.dot(taps1[...], window, preferred_element_type=F32)
        for r in range(BAND):
            i = start + r
            half = total[r * channels : (r + 1) * channels] + bias1
            value = half + half * jnp.tanh(half)
            if left is not None and i < HALO - 1:
                value = value * left
            if right is not None and i >= rows - 2 - (HALO - 1):
                value = value * right
            second[i] = value.astype(BF16)
    split = reach * channels
    for parity in range(2):
        for group in groups_of(run // 2):
            start = 2 * group + parity
            near = [first[start + 1 + 2 * i] for i in range(reach)]
            far = [second[start + 2 * i] for i in range(reach)]
            total = jnp.dot(
                taps2[:, :split], jnp.concatenate(near, axis=0), preferred_element_type=F32
            ) + jnp.dot(taps2[:, split:], jnp.concatenate(far, axis=0), preferred_element_type=F32)
            for r in range(BAND):
                n = start + 2 * r
                half = total[r * channels : (r + 1) * channels] + bias2
                third = (half + half * jnp.tanh(half)).astype(BF16).astype(F32)
                rest = jnp.sum(third * last, axis=0, keepdims=True)
                at = BAND * channels + r
                heads[n : n + 1, :] = total[at : at + 1] + rest


def in_runs(ext):
    run = (ext.shape[0] - 2 * HALO) // PARTS
    return jnp.concatenate([ext[q * run : (q + 1) * run + 2 * HALO] for q in range(PARTS)], axis=1)


def split3(value):
    one = value.astype(BF16)
    rest = value - one.astype(F32)
    two = rest.astype(BF16)
    three = (rest - two.astype(F32)).astype(BF16)
    return jnp.concatenate([one, two, three], axis=1)


def blank_kernel(blank):
    blank[...] = jnp.zeros_like(blank)


def end_masks(parts, members):
    space = lax.axis_index("space")
    lane = lax.broadcasted_iota(jnp.int32, (1, parts * members), 1)
    left = (lane < members) & (space == 0)
    right = (lane >= (parts - 1) * members) & (space == lax.axis_size("space") - 1)
    return jnp.where(left, 0.0, 1.0), jnp.where(right, 0.0, 1.0)


def prepare_kernel(
    empty, field, gain, bias, conv1, bias1, conv2, bias2, readout,
    obs_heads, obs_var, noise_turned, obs_index, obs_count,
    own, taps1, taps2, columns, sent,
    wide1, wide2, first, second, heads,
):
    space = lax.axis_index("space")
    spaces = lax.axis_size("space")
    turned = field[...].T
    own[...] = turned
    cells, members = turned.shape
    channels = gain.shape[0]
    row = readout[...].astype(F32).reshape(1, 3 * channels)
    split = (BAND + 2) * channels
    wide1[...] = jnp.zeros_like(wide1)
    wide2[...] = jnp.zeros_like(wide2)
    for tap in range(3):
        one = 0.5 * conv1[tap].astype(F32)
        both = 0.5 * conv2[tap].astype(F32)
        for r in range(BAND):
            out = slice(r * channels, (r + 1) * channels)
            at = (r + tap) * channels
            wide1[out, at : at + channels] = one
            wide2[out, at : at + channels] = both[:, :channels]
            wide2[out, split + at : split + at + channels] = both[:, channels:]
    for r in range(BAND):
        out, at = BAND * channels + r, (r + 1) * channels
        wide2[out : out + 1, at : at + channels] = row[:, :channels]
        wide2[out : out + 1, split + at : split + at + channels] = row[:, channels : 2 * channels]
    taps1[...] = wide1[...].astype(BF16)
    taps2[...] = wide2[...].astype(BF16)
    rows = [
        gain[...].reshape(1, channels),
        bias[...].reshape(1, channels),
        0.5 * bias1[...].reshape(1, channels),
        0.5 * bias2[...].reshape(1, channels),
        row[:, 2 * channels :],
    ]
    for spot, value in enumerate(rows):
        columns[spot] = jnp.broadcast_to(column(value), (channels, columns.shape[2]))
    slots = obs_var.shape[0]
    cell = obs_index[...]
    low_end = (cell < HALO) & (space > 0)
    high_end = (cell >= cells - HALO) & (space < spaces - 1)
    end_row = jnp.where(
        low_end,
        (space - 1) * EDGE + HALO + cell,
        jnp.where(high_end, space * EDGE + cell - (cells - HALO), -1),
    )
    inside = column(jnp.where(end_row < 0, cell, -1).astype(F32)).astype(jnp.int32)
    chosen = jnp.where(
        lax.broadcasted_iota(jnp.int32, (slots, cells), 1) == inside, 1.0, 0.0
    ).astype(BF16)
    variance = obs_var[...].reshape(1, slots)
    live = lax.broadcasted_iota(jnp.int32, (1, slots), 1) < obs_count[...].reshape(1, 1)
    root_row = jnp.where(live, lax.rsqrt(variance), 0.0)
    root = column(root_row)
    target = column(obs_heads[...].reshape(1, slots))
    goal = root * target
    noise = jnp.where(column(jnp.where(live, 1.0, 0.0)) > 0.0, noise_turned[...], 0.0)

    zeros = jnp.zeros((HALO, members), F32)
    wide = in_runs(jnp.concatenate([zeros, turned, zeros], axis=0))
    left, right = end_masks(PARTS, members)
    layers(wide, cells // PARTS, left, right, taps1, taps2, columns, first, second, heads)
    every = jnp.concatenate(
        [heads[:, q * members : (q + 1) * members] for q in range(PARTS)], axis=0
    )
    parts = jnp.dot(chosen, split3(every), preferred_element_type=F32)
    seen = parts[:, :members] + parts[:, members : 2 * members] + parts[:, 2 * members :]
    gap = goal - root * seen
    gap_high = gap.astype(BF16).astype(F32)
    root_high = root_row.astype(BF16).astype(F32)
    ends = jnp.concatenate([turned[: 2 * HALO], turned[cells - 2 * HALO :]], axis=1)
    ends_high = ends.astype(BF16).astype(F32)
    row_high = (end_row >> 6) << 6
    blank = empty[0:1, slots : 2 * members]
    payload = jnp.concatenate(
        [
            jnp.concatenate([gap_high, gap - gap_high], axis=1),
            jnp.concatenate([noise[: slots // 2], noise[slots // 2 :]], axis=1),
            ends_high,
            jnp.concatenate([row_high.astype(F32), blank], axis=1),
            jnp.concatenate([root_high, blank], axis=1),
            ends - ends_high,
            jnp.concatenate([(end_row - row_high).astype(F32), blank], axis=1),
            jnp.concatenate([root_row - root_high, blank], axis=1),
        ],
        axis=0,
    ).astype(BF16)
    for copy in range(sent.shape[0]):
        sent[copy] = payload


def tables_kernel(neighbours, near, near_turned, choice):
    members, order = neighbours.shape
    everyone = choice.shape[2]
    ids = neighbours[...] - members * lax.axis_index("members")
    ids = jnp.where(ids < 0, ids + everyone, ids)
    pair = jnp.concatenate([ids, ids], axis=1)
    table = jnp.concatenate([pair, pair], axis=0)
    near[...] = table
    turned = pair.T[:order]
    near_turned[...] = jnp.concatenate([turned, turned], axis=1)
    second_half = (lax.broadcasted_iota(jnp.int32, (128, 128), 0) >= 64).astype(jnp.int32)
    everyone_id = lax.broadcasted_iota(jnp.int32, (128, everyone), 1)
    for two in range(order // 2):
        member = jnp.take_along_axis(
            table, 2 * two + second_half, axis=1, mode="promise_in_bounds"
        )
        member = jnp.concatenate([member] * (everyone // 128), axis=1)
        choice[two] = jnp.where(member == everyone_id, 1.0, 0.0).astype(BF16)


def ends_kernel(
    got, own, taps1, taps2, columns,
    kept, swapped, first, second, heads, ends, marks, tails,
):
    space = lax.axis_index("space")
    spaces = got.shape[0]
    slots = (got.shape[1] - 2 * EDGE) * 2 // 3
    members = got.shape[2] // 2
    inner = 2 * HALO
    edge = slots + slots // 2
    for tile in range(spaces):
        pair = got[tile].astype(F32)[edge:]
        tails[tile] = pair[:EDGE] + pair[EDGE:]
    ends[...] = jnp.zeros_like(ends)
    for start in range(0, spaces, PARTS):
        sides = []
        for here in range(start, start + PARTS):
            there = (here + 1) % spaces
            near_end = tails[here, :inner, members:]
            far_end = tails[there, :inner, :members]
            sides.append(jnp.concatenate([near_end, far_end], axis=0))
        wide = jnp.concatenate(sides, axis=1)
        turn = start // PARTS
        layers(
            wide, inner, None, None, taps1, taps2, columns,
            first.at[turn], second.at[turn], heads.at[turn],
        )
        for q in range(PARTS):
            at = (start + q) * EDGE
            ends[at : at + inner, :] = heads[turn, :inner, q * members : (q + 1) * members]
    for tile in range(spaces):
        at = tile * slots
        marks[0:2, at : at + slots] = tails[tile, inner : inner + 2, :slots]
    row = lax.broadcasted_iota(jnp.int32, (spaces * EDGE, spaces * slots), 0).astype(F32)
    picks = jnp.where(row == marks[0:1, :], marks[1:2, :], 0.0)
    added = lax.dot_general(
        picks, jnp.concatenate([ends[...]] * 2, axis=1), (((0,), (0,)), ((), ())),
        precision=lax.Precision.HIGHEST, preferred_element_type=F32,
    )
    heads_lane = lax.broadcasted_iota(jnp.int32, (1, 2 * members), 1) < members
    half = spaces * slots // 2

    def finished(tile):
        at = slice(tile * slots, (tile + 1) * slots)
        there = got[tile].astype(F32)
        gap = there[:slots] + pltpu.roll(there[:slots], members, 1) - added[at]
        noise = there[slots:edge]
        noise = jnp.concatenate([pltpu.roll(noise, members, 1), noise], axis=0)
        return jnp.where(heads_lane, gap, gap + noise)

    for tile in range(spaces // 2):
        at = slice(tile * slots, (tile + 1) * slots)
        one, two = finished(tile), finished(tile + spaces // 2)
        kept[at, :] = one
        kept[half + tile * slots : half + (tile + 1) * slots, :] = two
        swapped[at, :] = jnp.where(heads_lane, one, pltpu.roll(two, members, 1))
    before = jnp.where(space == 0, spaces - 1, space - 1)
    after = jnp.where(space == spaces - 1, 0, space + 1)
    swapped[half : half + EDGE, :] = tails[before]
    swapped[half + EDGE : half + 2 * EDGE, :] = tails[after]
    middle = own.shape[0] // 2
    swapped[half + 2 * EDGE :, :] = jnp.concatenate([own[:middle, :], own[middle:, :]], axis=1)


def lane_gather(table, index):
    low = index & 127
    high = index >> 7
    found = None
    for tile in range(table.shape[1] // 128):
        part = jnp.take_along_axis(
            table[:, tile * 128 : (tile + 1) * 128], low, axis=1, mode="promise_in_bounds"
        )
        found = part if found is None else jnp.where(high == tile, part, found)
    return found


def update_kernel(groups, *refs):
    kept, parcels = refs[0], refs[1 : 1 + groups]
    (
        taps1, taps2, columns, near, near_turned, choice,
        updated, new_heads,
        system, first, second, heads, turned,
    ) = refs[1 + groups :]
    cells = updated.shape[1]
    slots, members = kept.shape[0], kept.shape[1] // 2
    everyone = groups * members
    order = near.shape[0] // 2
    half_lane = lax.broadcasted_iota(jnp.int32, (1, 128), 1) < 64

    panel = []
    for g in range(0, groups, 2):
        right = parcels[g + 1][0 : slots // 2, :]
        right = jnp.concatenate([pltpu.roll(right, members, 1), right], axis=0)
        if g:
            left = parcels[g][0 : slots // 2, :]
            left = jnp.concatenate([left, pltpu.roll(left, members, 1)], axis=0)
        else:
            left = kept[...]
        panel.append(jnp.where(half_lane, left, right))
    panel = jnp.concatenate(panel, axis=1)
    panel = panel - jnp.mean(panel, axis=1, keepdims=True)
    innovation = kept[:, members:]
    stacked = jnp.concatenate([panel, innovation], axis=1)
    product = lax.dot_general(
        stacked, panel, (((0,), (0,)), ((), ())),
        precision=lax.Precision.HIGHEST, preferred_element_type=F32,
    )
    gram = split3(product[:everyone])
    gram = jnp.concatenate(
        [gram[:, i * everyone : (i + 1) * everyone] for i in range(3)], axis=0
    )
    sides = -product[everyone:]

    ids = near[...]
    lane_id = lax.broadcasted_iota(jnp.int32, (128, 128), 1)
    row_id = lax.broadcasted_iota(jnp.int32, (128, 128), 0)

    def extract(quad, carry):
        found = []
        for b in range(2):
            one_hot = choice[2 * quad + b]
            rows = jnp.dot(
                jnp.concatenate([one_hot] * 3, axis=1), gram, preferred_element_type=F32
            )
            found.append(lane_gather(rows, ids))
        block = jnp.where(half_lane, found[0], found[1]).T
        own = 4 * quad + 2 * (row_id >= 64).astype(jnp.int32) + (lane_id >= 64).astype(jnp.int32)
        block = block + jnp.where((row_id & 63) == own, order - 1.0, 0.0)
        system[pl.ds(pl.multiple_of(quad * 128, 128), 128), :] = block
        return carry

    lax.fori_loop(0, order // 4, extract, 0, unroll=order // 4)
    side = lane_gather(jnp.concatenate([sides, sides], axis=0), ids)
    side = jnp.where(row_id >= 64, 1.0, side).T[:order]
    system[order // 2 * order : (order // 2 + 1) * order, :] = side

    blocks = order // 2
    def both(value):
        turn = pltpu.roll(value, 64, 1)
        return jnp.where(half_lane, value, turn), jnp.where(half_lane, turn, value)

    def without(value, pair):
        at = 2 * pair // 8 * 8
        row = lax.broadcasted_iota(jnp.int32, (8, 128), 0) + at
        tile = jnp.where((row >= 2 * pair) & (row < 2 * pair + 2), 0.0, value[at : at + 8])
        parts = [value[:at], tile, value[at + 8 :]]
        return jnp.concatenate([part for part in parts if part.shape[0]], axis=0)

    def factors(col0, col1, pair):
        one, two = 2 * pair, 2 * pair + 1
        d, e, f = col0[one:two], col1[one:two], col1[two : two + 1]
        inv = 1.0 / (d * f - e * e)
        fac0 = without((col0 * f - col1 * e) * inv, pair)
        fac1 = without((col1 * d - col0 * e) * inv, pair)
        return fac0, fac1, (f * inv, d * inv, e * inv)

    own_share, cross_share = [], []
    fac0, fac1, shares = factors(*both(system[0:order, :]), 0)
    for pair in range(blocks):
        own_share += [shares[0], shares[1]]
        cross_share += [shares[2], shares[2]]
        one, two = 2 * pair, 2 * pair + 1
        if pair + 1 < blocks:
            col0, col1 = both(system[(pair + 1) * order : (pair + 2) * order, :])
            later = factors(
                col0 - fac0 * col0[one:two] - fac1 * col0[two : two + 1],
                col1 - fac0 * col1[one:two] - fac1 * col1[two : two + 1],
                pair + 1,
            )
        for block in range(min(pair + 2, blocks), blocks + 1):
            at = block * order
            row0 = system[at + one : at + two, :]
            row1 = system[at + two : at + two + 1, :]
            system[at : at + order, :] = system[at : at + order, :] - fac0 * row0 - fac1 * row1
        if pair + 1 < blocks:
            fac0, fac1, shares = later
    sides = system[blocks * order :, :]
    even = lax.broadcasted_iota(jnp.int32, (order, 128), 0) % 2 == 0
    partner = jnp.where(even, pltpu.roll(sides, order - 1, 0), pltpu.roll(sides, 1, 0))
    solved = sides * jnp.concatenate(own_share, axis=0) - partner * jnp.concatenate(
        cross_share, axis=0
    )
    sums = jnp.sum(solved, axis=0, keepdims=True)
    share = sums / pltpu.roll(sums, 64, 1)
    coef = (solved - pltpu.roll(solved, 64, 1) * share)[:, :members]
    coef = coef - jnp.mean(coef, axis=0, keepdims=True)
    coef = jnp.concatenate([coef, coef], axis=1)
    name = lax.broadcasted_iota(jnp.int32, (everyone // 2, 128), 0) + jnp.where(
        half_lane, 0, everyone // 2
    )
    mixing = jnp.zeros((everyone // 2, 128), F32)
    for i in range(order):
        mixing = jnp.where(name == near_turned[i : i + 1, :], coef[i : i + 1], mixing)
    mixing = jnp.concatenate([mixing[:, :members], mixing[:, members:]], axis=0)

    before = slots // 2
    after, body = before + EDGE, before + 2 * EDGE
    sources = jnp.concatenate(
        [
            jnp.concatenate([full[before + HALO : before + 2 * HALO, members:] for full in parcels], axis=1),
            jnp.concatenate([full[body:, :members] for full in parcels], axis=1),
            jnp.concatenate([full[body:, members:] for full in parcels], axis=1),
            jnp.concatenate([full[after : after + HALO, :members] for full in parcels], axis=1),
        ],
        axis=0,
    )
    field = sources[:, :members] + jnp.dot(
        sources, mixing, precision=lax.Precision.HIGHEST, preferred_element_type=F32
    )
    updated[...] = field[HALO : HALO + cells].T
    run = cells // PARTS
    left, right = end_masks(PARTS, members)
    layers(in_runs(field), run, left, right, taps1, taps2, columns, first, second, heads)
    for q in range(PARTS):
        turned[q * run : (q + 1) * run, :] = heads[:, q * members : (q + 1) * members]
    new_heads[...] = turned[...].T


def from_groups(value):
    groups = lax.axis_size("members")
    found = [value]
    for step in range(1, groups):
        pairs = [((i + step) % groups, i) for i in range(groups)]
        found.append(lax.ppermute(value, "members", pairs))
    return found


def on_device(
    log_field, obs_heads, obs_var, obs_noise, obs_index, obs_count, neighbours,
    lift_gain, lift_bias, conv_first, bias_first, conv_second, bias_second, readout,
):
    members, cells = log_field.shape
    spaces = lax.axis_size("space")
    groups = lax.axis_size("members")
    channels = lift_gain.shape[0]
    slots = obs_var.shape[0]
    order = neighbours.shape[1]

    def work(run, parts):
        rows, lanes = run + 2 * HALO, parts * members
        return (
            pltpu.VMEM((rows, channels, lanes), BF16),
            pltpu.VMEM((rows - 2, channels, lanes), BF16),
            pltpu.VMEM((max(run, 8), lanes), F32),
        )

    reach = (BAND + 2) * channels
    empty = call(blank_kernel, shape((8, 2 * members)), (), flops=1 << 34)
    own, taps1, taps2, columns, sent = call(
        prepare_kernel,
        (
            shape((cells, members)),
            shape((BAND * channels, reach), BF16),
            shape((BAND * channels + 16, 2 * reach), BF16),
            shape((5, channels, 128)),
            shape((spaces, slots + slots // 2 + 2 * EDGE, 2 * members), BF16),
        ),
        (
            empty, log_field, lift_gain, lift_bias, conv_first, bias_first, conv_second, bias_second,
            readout, obs_heads, obs_var, obs_noise.T, obs_index, obs_count,
        ),
        scratch=(
            pltpu.VMEM((BAND * channels, reach), F32),
            pltpu.VMEM((BAND * channels + 16, 2 * reach), F32),
        )
        + work(cells // PARTS, PARTS),
    )
    got = lax.all_to_all(sent, "space", 0, 0)
    near, near_turned, choice = call(
        tables_kernel,
        (
            shape((2 * members, 2 * order), jnp.int32),
            shape((order, 2 * members), jnp.int32),
            shape((order // 2, 2 * members, groups * members), BF16),
        ),
        (neighbours,),
        flops=1 << 30,
    )
    turns = spaces // PARTS
    kept, swapped = call(
        ends_kernel,
        (
            shape((spaces * slots, 2 * members)),
            shape((spaces * slots // 2 + 2 * EDGE + cells // 2, 2 * members)),
        ),
        (got, own, taps1, taps2, columns),
        scratch=tuple(
            pltpu.VMEM((turns, *value.shape), value.dtype) for value in work(2 * HALO, PARTS)
        )
        + (
            pltpu.VMEM((spaces * EDGE, members), F32),
            pltpu.VMEM((8, spaces * slots), F32),
            pltpu.VMEM((spaces, EDGE, 2 * members), F32),
        ),
    )
    return call(
        functools.partial(update_kernel, groups),
        (shape((members, cells)), shape((members, cells))),
        (kept, *from_groups(swapped), taps1, taps2, columns, near, near_turned, choice),
        scratch=(pltpu.VMEM(((order // 2 + 1) * order, 128), F32),)
        + work(cells // PARTS, PARTS)
        + (pltpu.VMEM((cells, members), F32),),
    )


def solution(mesh):
    in_specs = (
        P("members", "space"),
        P("space"),
        P("space"),
        P("members", "space"),
        P("space", None),
        P("space"),
        P("members", None),
        P(),
        P(),
        P(),
        P(),
        P(),
        P(),
        P(),
    )
    out_specs = (P("members", "space"), P("members", "space"))
    return jax.shard_map(
        on_device, mesh=mesh, in_specs=in_specs, out_specs=out_specs, check_vma=False
    )
```
